128 devices in a mesh: grp: 8 (over z, core), frac: 16 (over y, x).
Axes of the slice: x: 4, y: 4, z: 4, core: 2. Of those that a mesh axis runs over, the one named last changes fastest.
Arguments:
- matrix_state: float32 [2, 1024, 4096], P(None, 'grp', 'frac'), may hold values from 0 to 1
- matrix_perm: float32 [1024, 4096], P('grp', 'frac'), may hold values from 0.1 to 10
- frac_state: float32 [2, 8, 131072], P(None, 'grp', 'frac'), may hold values from 0 to 1
- frac_aperture: float32 [8, 131072], P('grp', 'frac'), may hold values from 0.5 to 4
- link_cell: int32 [8, 16, 16, 256], P('grp', 'frac'), may hold values from 0 to 32767
- link_seg: int32 [8, 16, 16, 256], P('grp', 'frac'), may hold values from 0 to 8191
- link_trans: float32 [8, 16, 16, 256], P('grp', 'frac'), may hold values from 0.1 to 2
- link_count: int32 [8, 16, 16], P('grp', 'frac'), may hold values from 32 to 256, as said below
- link_upwind: int32 [3, 8, 16, 16, 256], P(None, 'grp', 'frac'), may hold values from 0 to 1
Outputs:
- matrix_out: float32 [2, 1024, 4096], P(None, 'grp', 'frac')
- frac_out: float32 [2, 8, 131072], P(None, 'grp', 'frac')
The draws below stay inside these ranges and needn't reach their ends.
Inputs may be any that keep to these rules, and one draw needn't show every extreme that they name: `link_count`: in each source device's list at least one owner block holds exactly 256 live slots; slots at or beyond a block's count are padding. `link_cell`: A live slot's cell index lies within the source device's 128 x 256 block. `link_seg`: A slot's segment index counts within the owner's 8192 segments. `link_upwind`: 1 takes the upwind saturation from the matrix cell, 0 from the fracture segment.
All inputs are finite; a program needn't handle non-finite values.
Results may differ from the reference program's by a relative error of at most 0.00002.
Values sent between devices are 32-bit elements; how exact they have to be, the bound alone decides.
A program may use at most 128 MiB of HBM per device.

```python
import math
import jax
import jax.numpy as jnp

CR = 128
CC = 256
SEG_DEV = 8192
CAP = 256
ITERS = 3
SWEEPS = 4
GROUPS = 8
MEMBERS = 16
NR = 1024
NC = 4096
SEG = 131072


def draw_link_count(key, part):
    first_key, second_key = jax.random.split(jax.random.fold_in(key, 17))
    lowest = max(1, CAP // 8)
    base_counts = jax.random.randint(first_key, (GROUPS, MEMBERS, MEMBERS), lowest, CAP + 1)
    full_owner = jax.random.randint(second_key, (GROUPS, MEMBERS, 1), 0, MEMBERS)
    owner_ids = jnp.arange(MEMBERS, dtype=jnp.int32)[None, None, :]
    return jnp.where(owner_ids == full_owner, CAP, base_counts).astype(jnp.int32)


def with_ends(array, rng, smallest, largest):
    longest = array.shape.index(max(array.shape))
    spots = []
    for shift in (0, 1):
        where = [jax.random.randint(jax.random.fold_in(rng, axis), (), 0, length) for axis, length in enumerate(array.shape)]
        where[longest] = (where[longest] + shift) % array.shape[longest]
        spots.append(tuple(where))
    return array.at[spots[0]].set(smallest).at[spots[1]].set(largest)


def steps_of(key, shape, cuts, low, largest):
    gain, own = 1.0, jax.random.fold_in(key, 6)
    for axis_at, parts in cuts:
        heights = jnp.exp(jax.random.uniform(jax.random.fold_in(own, axis_at), (parts,), jnp.float32, low / len(cuts), largest / len(cuts)))
        gain = gain * jnp.repeat(heights, shape[axis_at] // parts).reshape([-1 if axis == axis_at else 1 for axis in range(len(shape))])
    return gain


def setup_inputs(seed: int = 0) -> dict:
    splits = jax.random.split(jax.random.key(seed), 10)
    return {
        "matrix_state": jnp.clip(1.0 * jax.random.uniform(splits[0], (2, NR, NC), jnp.float32) ** steps_of(splits[0], (2, NR, NC), ((1, 8), (2, 16)), -0.2, 0.2), 0.0, 1.0),
        "matrix_perm": jnp.clip(jnp.exp(math.log(10.0) - 4.6051702 * jax.random.uniform(splits[1], (NR, NC), jnp.float32) ** steps_of(splits[1], (NR, NC), ((0, 8), (1, 16)), -0.2, 0.2)), 0.1, 10.0),
        "frac_state": jnp.clip(1.0 * jax.random.uniform(splits[2], (2, GROUPS, SEG), jnp.float32) ** steps_of(splits[2], (2, GROUPS, SEG), ((1, 8), (2, 16)), -0.2, 0.2), 0.0, 1.0),
        "frac_aperture": jnp.clip(jnp.exp(math.log(4.0) - 2.0794415 * jax.random.uniform(splits[3], (GROUPS, SEG), jnp.float32) ** steps_of(splits[3], (GROUPS, SEG), ((0, 8), (1, 16)), -0.2, 0.2)), 0.5, 4.0),
        "link_cell": with_ends(jax.random.randint(splits[4], (GROUPS, MEMBERS, MEMBERS, CAP), 0, CR * CC), jax.random.fold_in(splits[4], 1), 0, (CR * CC) - 1).astype(jnp.int32),
        "link_seg": with_ends(jax.random.randint(splits[5], (GROUPS, MEMBERS, MEMBERS, CAP), 0, SEG_DEV), jax.random.fold_in(splits[5], 1), 0, SEG_DEV - 1).astype(jnp.int32),
        "link_trans": jnp.clip(jnp.exp(math.log(2.0) - 2.9957323 * jax.random.uniform(splits[6], (GROUPS, MEMBERS, MEMBERS, CAP), jnp.float32) ** steps_of(splits[6], (GROUPS, MEMBERS, MEMBERS, CAP), ((0, 8), (1, 16)), -0.2, 0.2)), 0.1, 2.0),
        "link_count": draw_link_count(jax.random.fold_in(splits[9], 71), 0),
        "link_upwind": with_ends(jax.random.randint(splits[8], (ITERS, GROUPS, MEMBERS, MEMBERS, CAP), 0, 2), jax.random.fold_in(splits[8], 1), 0, 1).astype(jnp.int32),
    }


LOW_BOUND = 0.02
HIGH_BOUND = 1.98
TAU_STEP = 0.5
MOBILITY_FLOOR = 0.2


def apply_matrix(values, diagonal):
    padded = jnp.pad(values, 1)
    beside = padded[2:, 1:-1] + padded[:-2, 1:-1] + padded[1:-1, 2:] + padded[1:-1, :-2]
    return diagonal * values - beside


def chebyshev(start_field, right_side, diagonal):
    centre = 0.5 * (HIGH_BOUND + LOW_BOUND)
    half_width = 0.5 * (HIGH_BOUND - LOW_BOUND)
    scale_ratio = centre / half_width
    ratio_now = 1.0 / scale_ratio
    inverse = 1.0 / diagonal
    residual = inverse * (right_side - apply_matrix(start_field, diagonal))
    update = residual / centre
    iterate = start_field
    for sweep_index in range(SWEEPS):
        iterate = iterate + update
        if sweep_index + 1 < SWEEPS:
            residual = inverse * (right_side - apply_matrix(iterate, diagonal))
            ratio_next = 1.0 / (2.0 * scale_ratio - ratio_now)
            update = ratio_next * ratio_now * update + (2.0 * ratio_next / half_width) * residual
            ratio_now = ratio_next
    return iterate


def reference(matrix_state, matrix_perm, frac_state, frac_aperture, link_cell, link_seg, link_trans, link_count, link_upwind):
    shape_all = link_cell.shape
    group_ids = jnp.broadcast_to(jnp.arange(GROUPS, dtype=jnp.int32)[:, None, None, None], shape_all)
    source_ids = jnp.arange(MEMBERS, dtype=jnp.int32)[None, :, None, None]
    owner_ids = jnp.arange(MEMBERS, dtype=jnp.int32)[None, None, :, None]
    slot_ids = jnp.arange(CAP, dtype=jnp.int32)[None, None, None, :]
    live_slots = (slot_ids < link_count[..., None]).astype(jnp.int32)
    row_index = group_ids * CR + link_cell // CC
    column_index = jnp.broadcast_to(source_ids * CC + link_cell % CC, shape_all)
    segment_index = jnp.broadcast_to(owner_ids * SEG_DEV + link_seg, shape_all)
    pressure = matrix_state[0]
    saturation = matrix_state[1]
    frac_pressure = frac_state[0]
    frac_saturation = frac_state[1]
    for outer in range(ITERS):
        cell_pressure = pressure[row_index, column_index]
        cell_saturation = saturation[row_index, column_index]
        seg_pressure = frac_pressure[group_ids, segment_index]
        seg_saturation = frac_saturation[group_ids, segment_index]
        upwind_sat = jnp.where(link_upwind[outer] == 1, cell_saturation, seg_saturation)
        weight = jnp.where(live_slots == 1, link_trans * (MOBILITY_FLOOR + upwind_sat * upwind_sat), jnp.float32(0.0))
        water_flux = weight * (cell_pressure - seg_pressure) * upwind_sat
        empty_cells = jnp.zeros((NR, NC), jnp.float32)
        couple = empty_cells.at[row_index, column_index].add(weight)
        source_term = empty_cells.at[row_index, column_index].add(weight * seg_pressure)
        water_lost = empty_cells.at[row_index, column_index].add(water_flux)
        empty_segs = jnp.zeros((GROUPS, SEG), jnp.float32)
        inflow = empty_segs.at[group_ids, segment_index].add(weight * cell_pressure)
        weight_total = empty_segs.at[group_ids, segment_index].add(weight)
        gained = empty_segs.at[group_ids, segment_index].add(water_flux)
        diagonal = 4.0 + matrix_perm + couple
        new_pressure = chebyshev(pressure, matrix_perm * pressure + source_term, diagonal)
        new_saturation = saturation - TAU_STEP * water_lost / (matrix_perm + couple)
        left_values = jnp.pad(frac_pressure, ((0, 0), (1, 0)))[:, :-1]
        right_values = jnp.pad(frac_pressure, ((0, 0), (0, 1)))[:, 1:]
        new_frac_pressure = (frac_aperture * frac_pressure + inflow + left_values + right_values) / (frac_aperture + weight_total + 2.0)
        new_frac_saturation = frac_saturation + TAU_STEP * gained / (frac_aperture + weight_total)
        pressure = new_pressure
        saturation = new_saturation
        frac_pressure = new_frac_pressure
        frac_saturation = new_frac_saturation
    return jnp.stack([pressure, saturation]), jnp.stack([frac_pressure, frac_saturation])
```

```python
import functools

import jax
import jax.numpy as jnp
from jax import lax
from jax.experimental import pallas as pl
from jax.experimental.pallas import tpu as pltpu
from jax.sharding import PartitionSpec as P

ITERS = 3
SWEEPS = 4
LOW_BOUND = 0.02
HIGH_BOUND = 1.98
TAU_STEP = 0.5
MOBILITY_FLOOR = 0.2

F32 = jnp.float32
BF16 = jnp.bfloat16
MESH = pl.DeviceIdType.MESH
LANES = 128
ROWS = 8
AROUND = ((-1, 0), (1, 0), (0, -1), (0, 1), (-1, -1), (-1, 1), (1, -1), (1, 1))


def pieces(value):
    high = value.astype(BF16)
    low = (value - high.astype(F32)).astype(BF16)
    return high, low


def one_hot(index, count):
    ids = lax.broadcasted_iota(jnp.int32, (count, index.shape[1]), 0)
    return jnp.where(ids == index, F32(1.0), F32(0.0)).astype(BF16)


def spread(hot, values):
    rows, count = hot.shape
    stacked = hot.reshape(rows // 16, 16, count)
    out = []
    for value in values:
        for part in pieces(jnp.broadcast_to(value, (16, count))):
            out.append((stacked * part[None]).reshape(rows, count))
    return jnp.concatenate(out, axis=0)


def flux_terms(trans, upwind, cell_p, cell_s, seg_p, seg_s):
    u = jnp.where(upwind > 0.5, cell_s, seg_s)
    weight = trans * (MOBILITY_FLOOR + u * u)
    return weight, weight * (cell_p - seg_p) * u


def kernel(
    groups,
    members,
    cap,
    state_ref,
    perm_ref,
    frac_ref,
    aperture_ref,
    cell_ref,
    seg_ref,
    trans_ref,
    count_ref,
    upwind_ref,
    matrix_out,
    frac_out,
    stat_send,
    stat_recv,
    p_send,
    p_recv,
    f_send,
    f_recv,
    edge_left,
    edge_right,
    fields,
    sat,
    fq,
    side_send,
    halo_row,
    halo_col,
    col_hot,
    row_hot,
    low_hot,
    high_hot,
    cell_acc,
    seg_acc,
    ext_x,
    ext_inv,
    ext_c,
    stat_ss,
    stat_rs,
    p_ss,
    p_rs,
    f_ss,
    f_rs,
    edge_ss,
    edge_rs,
    halo_ss,
    halo_rs,
):
    g = lax.axis_index("grp")
    me = lax.axis_index("frac")
    slots = members * cap
    rows, cols = perm_ref.shape
    seg_rows = aperture_ref.shape[0]
    group = min(slots, 4 * cap)

    def member(step):
        return lax.rem(me + step + members, members)

    def neighbour(step):
        return (lax.rem(g + step[0] + groups, groups), member(step[1]))

    barrier = pltpu.get_barrier_semaphore()
    for k in range(1, members):
        pl.semaphore_signal(barrier, inc=1, device_id=(g, member(k)), device_id_type=MESH)
    apart = [step for step in AROUND if step[0] != 0]
    for step in apart:
        pl.semaphore_signal(barrier, inc=1, device_id=neighbour(step), device_id_type=MESH)

    def lanes(block, width):
        return pl.ds(pl.multiple_of(block * width, width), width)

    eye = lax.broadcasted_iota(jnp.int32, (members, members), 0) == lax.broadcasted_iota(
        jnp.int32, (members, members), 1
    )
    counts = jnp.sum(
        jnp.where(eye, jnp.broadcast_to(count_ref[...].astype(F32), (members, members)), 0.0),
        axis=1,
        keepdims=True,
    )
    place = lax.broadcasted_iota(jnp.int32, (members, cap), 1).astype(F32)
    live_trans = jnp.where(place < counts, trans_ref[...], F32(0.0))
    seg_float = seg_ref[...].astype(F32)
    ups = [upwind_ref[t].astype(F32) for t in range(ITERS)]
    stat_send[...] = jnp.zeros_like(stat_send)
    for o in range(members):
        here = slice(o * cap, (o + 1) * cap)
        stat_send[0:1, here] = live_trans[o : o + 1, :]
        stat_send[1:2, here] = seg_float[o : o + 1, :]
        for t in range(ITERS):
            stat_send[2 + t : 3 + t, here] = ups[t][o : o + 1, :]

    pl.semaphore_wait(barrier, members - 1 + len(apart))

    def exchange(send, recv, send_sem, recv_sem, k):
        to = member(k)
        return pltpu.make_async_remote_copy(
            src_ref=send.at[:, lanes(to, cap)],
            dst_ref=recv.at[:, lanes(me, cap)],
            send_sem=send_sem,
            recv_sem=recv_sem,
            device_id=(g, to),
            device_id_type=MESH,
        )

    def stat_copy(k):
        return exchange(stat_send, stat_recv, stat_ss.at[k], stat_rs.at[k], k)

    def p_copy(t, k):
        return exchange(p_send.at[t], p_recv.at[t], p_ss.at[t, k], p_rs.at[t, k], k)

    def f_copy(t, k):
        return exchange(f_send.at[t], f_recv.at[t], f_ss.at[t, k], f_rs.at[t, k], k)

    def each(body):
        lax.fori_loop(1, members, lambda k, c: (body(k), c)[1], 0)

    each(lambda k: stat_copy(k).start())
    stat_recv[:, lanes(me, cap)] = stat_send[:, lanes(me, cap)]

    def edge_copies(t):
        return (
            pltpu.make_async_remote_copy(
                src_ref=fq.at[t, 0, pl.ds(seg_rows - ROWS, ROWS), :],
                dst_ref=edge_left.at[t],
                send_sem=edge_ss.at[t, 0],
                recv_sem=edge_rs.at[t, 0],
                device_id=(g, member(1)),
                device_id_type=MESH,
            ),
            pltpu.make_async_remote_copy(
                src_ref=fq.at[t, 0, pl.ds(0, ROWS), :],
                dst_ref=edge_right.at[t],
                send_sem=edge_ss.at[t, 1],
                recv_sem=edge_rs.at[t, 1],
                device_id=(g, member(-1)),
                device_id_type=MESH,
            ),
        )

    def halo_copies(t):
        out = []
        for i, (dr, dc) in enumerate(AROUND):
            if dr == 0:
                src = side_send.at[t, i - 2]
                dst = halo_col.at[t, i - 2]
            else:
                edge = pl.ds(0 if dr < 0 else rows - ROWS, ROWS)
                if dc == 0:
                    src = fields.at[t, :, edge, :]
                    dst = halo_row.at[t, i]
                else:
                    src = fields.at[t, :, edge, pl.ds(0 if dc < 0 else cols - LANES, LANES)]
                    dst = halo_col.at[t, i - 2]
            out.append(
                pltpu.make_async_remote_copy(
                    src_ref=src,
                    dst_ref=dst,
                    send_sem=halo_ss.at[t, i],
                    recv_sem=halo_rs.at[t, i],
                    device_id=neighbour((dr, dc)),
                    device_id_type=MESH,
                )
            )
        return out

    fields[0, 0] = state_ref[0]
    sat[...] = state_ref[1]
    fq[0] = frac_ref[...]

    def cell_hots(o, carry):
        index = cell_ref[pl.ds(o, 1), :]
        col_hot[:, lanes(o, cap)] = one_hot(lax.rem(index, cols), cols)
        row_hot[:, lanes(o, cap)] = one_hot(lax.div(index, cols), rows)
        return carry

    lax.fori_loop(0, members, cell_hots, 0)

    each(lambda k: stat_copy(k).wait_recv())

    def seg_hots(o, carry):
        index = stat_recv[1:2, lanes(o, cap)].astype(jnp.int32)
        low_hot[:, lanes(o, cap)] = one_hot(lax.rem(index, LANES), LANES)
        high_hot[:, lanes(o, cap)] = one_hot(lax.div(index, LANES), seg_rows)
        return carry

    lax.fori_loop(0, members, seg_hots, 0)

    def gather_segments(t):
        for copy in edge_copies(t):
            copy.start()
        table = jnp.concatenate(
            [jnp.concatenate(pieces(fq[t, f]), axis=1) for f in range(2)], axis=0
        )

        def body(k, carry):
            here = lanes(member(k), cap)
            low = low_hot[:, here]
            picked = jnp.dot(
                table, jnp.concatenate([low, low], axis=0), preferred_element_type=F32
            )
            high = high_hot[:, here].astype(F32)
            for f in range(2):
                value = jnp.sum(
                    picked[f * seg_rows : (f + 1) * seg_rows] * high, axis=0, keepdims=True
                )
                f_send[t, f : f + 1, here] = value

                @pl.when(k == 0)
                def _():
                    f_recv[t, f : f + 1, here] = value

            @pl.when(k > 0)
            def _():
                f_copy(t, k).start()

            return carry

        lax.fori_loop(0, members, body, 0)

    def gather_cells(t):
        table = jnp.concatenate(pieces(fields[t, 0]) + pieces(sat[...]), axis=0)

        def body(k, carry):
            here = lanes(member(k), cap)
            picked = jnp.dot(table, col_hot[:, here], preferred_element_type=F32)
            hot = row_hot[:, here].astype(F32)
            for f in range(2):
                both = (
                    picked[2 * f * rows : (2 * f + 1) * rows]
                    + picked[(2 * f + 1) * rows : (2 * f + 2) * rows]
                )
                value = jnp.sum(both * hot, axis=0, keepdims=True)
                p_send[t, f : f + 1, here] = value

                @pl.when(k == 0)
                def _():
                    p_recv[t, f : f + 1, here] = value

            @pl.when(k > 0)
            def _():
                p_copy(t, k).start()

            return carry

        lax.fori_loop(0, members, body, 0)

    def collect(acc, hot_rows, hot_cols, values_of):
        acc[...] = jnp.zeros_like(acc)

        def body(j, carry):
            here = lanes(j, group)
            left = spread(hot_rows[:, here], values_of(here))
            acc[...] += lax.dot_general(
                left, hot_cols[:, here], (((1,), (1,)), ((), ())), preferred_element_type=F32
            )
            return carry

        lax.fori_loop(0, slots // group, body, 0)
        height = hot_rows.shape[0]
        return [
            acc[2 * f * height : (2 * f + 1) * height]
            + acc[(2 * f + 1) * height : (2 * f + 2) * height]
            for f in range(3)
        ]

    def scatter_cells(t):
        def values_of(here):
            seg_p = f_recv[t, 0:1, here]
            weight, water = flux_terms(
                stat_send[0:1, here],
                stat_send[pl.ds(2 + t, 1), here],
                p_send[t, 0:1, here],
                p_send[t, 1:2, here],
                seg_p,
                f_recv[t, 1:2, here],
            )
            return weight, weight * seg_p, water

        couple, source, lost = collect(cell_acc, row_hot, col_hot, values_of)
        perm = perm_ref[...]
        p = fields[t, 0]
        inverse = 1.0 / (4.0 + perm + couple)
        scaled = inverse * (perm * p + source)
        sat[...] = sat[...] - TAU_STEP * lost / (perm + couple)
        fields[t, 1] = inverse
        fields[t, 2] = scaled
        for f, field in enumerate((p, inverse, scaled)):
            side_send[t, 0, f] = jnp.transpose(field[:, :LANES])[:ROWS]
            side_send[t, 1, f] = jnp.transpose(field[:, cols - LANES :])[LANES - ROWS :]

    def scatter_segments(t):
        def values_of(here):
            cell_p = p_recv[t, 0:1, here]
            weight, water = flux_terms(
                stat_recv[0:1, here],
                stat_recv[pl.ds(2 + t, 1), here],
                cell_p,
                p_recv[t, 1:2, here],
                f_send[t, 0:1, here],
                f_send[t, 1:2, here],
            )
            return weight * cell_p, weight, water

        inflow, total, gained = collect(seg_acc, high_hot, low_hot, values_of)
        for copy in edge_copies(t):
            copy.wait_recv()
        aperture = aperture_ref[...]
        p = fq[t, 0]
        first = jnp.where(me > 0, edge_left[t, ROWS - 1 : ROWS, LANES - 1 : LANES], F32(0.0))
        last = jnp.where(me < members - 1, edge_right[t, 0:1, 0:1], F32(0.0))
        lane = lax.broadcasted_iota(jnp.int32, (seg_rows, LANES), 1)
        row = lax.broadcasted_iota(jnp.int32, (seg_rows, LANES), 0)
        turned = pltpu.roll(p, 1, axis=1)
        left = jnp.where(lane == 0, pltpu.roll(turned, 1, axis=0), turned)
        left = jnp.where((lane == 0) & (row == 0), first, left)
        turned = pltpu.roll(p, LANES - 1, axis=1)
        right = jnp.where(lane == LANES - 1, pltpu.roll(turned, seg_rows - 1, axis=0), turned)
        right = jnp.where((lane == LANES - 1) & (row == seg_rows - 1), last, right)
        fq[t + 1, 0] = (aperture * p + inflow + left + right) / (aperture + total + 2.0)
        fq[t + 1, 1] = fq[t, 1] + TAU_STEP * gained / (aperture + total)

    def sweeps(t):
        for copy in halo_copies(t):
            copy.wait_recv()
        inside = {
            -1: jnp.where(g > 0, F32(1.0), F32(0.0)),
            1: jnp.where(g < groups - 1, F32(1.0), F32(0.0)),
            0: F32(1.0),
        }
        beside = {
            -1: jnp.where(me > 0, F32(1.0), F32(0.0)),
            1: jnp.where(me < members - 1, F32(1.0), F32(0.0)),
        }
        corner = {
            (-dr, -dc): i - 2 for i, (dr, dc) in enumerate(AROUND) if dc != 0
        }
        east = lax.broadcasted_iota(jnp.int32, (ROWS, LANES), 1) < LANES // 2
        filler = jnp.zeros((LANES - 2 * ROWS, LANES), F32)
        for f, ext in enumerate((ext_x, ext_inv, ext_c)):
            ext[0:ROWS, 0:cols] = halo_row[t, 1, f] * inside[-1]
            ext[ROWS : ROWS + rows, 0:cols] = fields[t, f]
            ext[ROWS + rows :, 0:cols] = halo_row[t, 0, f] * inside[1]
            for dr, at in ((-1, slice(0, ROWS)), (1, slice(ROWS + rows, rows + 2 * ROWS))):
                ext[at, cols:] = jnp.where(
                    east,
                    halo_col[t, corner[dr, 1], f] * (inside[dr] * beside[1]),
                    halo_col[t, corner[dr, -1], f] * (inside[dr] * beside[-1]),
                )
            ext[ROWS : ROWS + rows, cols:] = jnp.transpose(
                jnp.concatenate(
                    [
                        halo_col[t, corner[0, 1], f] * beside[1],
                        filler,
                        halo_col[t, corner[0, -1], f] * beside[-1],
                    ],
                    axis=0,
                )
            )

        height, width = ext_x.shape
        inverse = ext_inv[...]
        scaled = ext_c[...]

        def residual_of(x):
            around = (
                pltpu.roll(x, 1, axis=0)
                + pltpu.roll(x, height - 1, axis=0)
                + pltpu.roll(x, 1, axis=1)
                + pltpu.roll(x, width - 1, axis=1)
            )
            return inverse * around + (scaled - x)

        centre = 0.5 * (HIGH_BOUND + LOW_BOUND)
        half_width = 0.5 * (HIGH_BOUND - LOW_BOUND)
        scale_ratio = centre / half_width
        ratio_now = 1.0 / scale_ratio
        x = ext_x[...]
        update = residual_of(x) / centre
        for sweep_index in range(SWEEPS):
            x = x + update
            if sweep_index + 1 < SWEEPS:
                ratio_next = 1.0 / (2.0 * scale_ratio - ratio_now)
                update = ratio_next * ratio_now * update + (
                    2.0 * ratio_next / half_width
                ) * residual_of(x)
                ratio_now = ratio_next
        fields[t + 1, 0] = x[ROWS : ROWS + rows, :cols]

    gather_segments(0)

    def outer(t, carry):
        gather_cells(t)
        each(lambda k: f_copy(t, k).wait_recv())
        scatter_cells(t)
        for copy in halo_copies(t):
            copy.start()
        each(lambda k: p_copy(t, k).wait_recv())
        scatter_segments(t)

        @pl.when(t + 1 < ITERS)
        def _():
            gather_segments(t + 1)

        sweeps(t)
        return carry

    lax.fori_loop(0, ITERS, outer, 0)

    matrix_out[0] = fields[ITERS, 0]
    matrix_out[1] = sat[...]
    frac_out[...] = fq[ITERS]

    each(lambda k: stat_copy(k).wait_send())

    def drain(t, carry):
        each(lambda k: p_copy(t, k).wait_send())
        each(lambda k: f_copy(t, k).wait_send())
        for copy in edge_copies(t):
            copy.wait_send()
        for copy in halo_copies(t):
            copy.wait_send()
        return carry

    lax.fori_loop(0, ITERS, drain, 0)


def on_device(
    matrix_state,
    matrix_perm,
    frac_state,
    frac_aperture,
    link_cell,
    link_seg,
    link_trans,
    link_count,
    link_upwind,
):
    groups = lax.axis_size("grp")
    members, cap = link_cell.shape[2:]
    rows, cols = matrix_perm.shape
    segs = frac_aperture.shape[1]
    seg_rows = segs // LANES
    slots = members * cap
    vmem = pl.BlockSpec(memory_space=pltpu.VMEM)
    dma = pltpu.SemaphoreType.DMA
    around = len(AROUND)
    matrix_out, frac_out = pl.pallas_call(
        functools.partial(kernel, groups, members, cap),
        out_shape=(
            jax.ShapeDtypeStruct(matrix_state.shape, F32),
            jax.ShapeDtypeStruct((2, seg_rows, LANES), F32),
        ),
        in_specs=[vmem] * 9,
        out_specs=(vmem, vmem),
        scratch_shapes=[
            pltpu.VMEM((ROWS, slots), F32),
            pltpu.VMEM((ROWS, slots), F32),
            pltpu.VMEM((ITERS, 2, slots), F32),
            pltpu.VMEM((ITERS, 2, slots), F32),
            pltpu.VMEM((ITERS, 2, slots), F32),
            pltpu.VMEM((ITERS, 2, slots), F32),
            pltpu.VMEM((ITERS, ROWS, LANES), F32),
            pltpu.VMEM((ITERS, ROWS, LANES), F32),
            pltpu.VMEM((ITERS + 1, 3, rows, cols), F32),
            pltpu.VMEM((rows, cols), F32),
            pltpu.VMEM((ITERS + 1, 2, seg_rows, LANES), F32),
            pltpu.VMEM((ITERS, 2, 3, ROWS, LANES), F32),
            pltpu.VMEM((ITERS, 2, 3, ROWS, cols), F32),
            pltpu.VMEM((ITERS, 6, 3, ROWS, LANES), F32),
            pltpu.VMEM((cols, slots), BF16),
            pltpu.VMEM((rows, slots), BF16),
            pltpu.VMEM((LANES, slots), BF16),
            pltpu.VMEM((seg_rows, slots), BF16),
            pltpu.VMEM((6 * rows, cols), F32),
            pltpu.VMEM((6 * seg_rows, LANES), F32),
            pltpu.VMEM((rows + 2 * ROWS, cols + LANES), F32),
            pltpu.VMEM((rows + 2 * ROWS, cols + LANES), F32),
            pltpu.VMEM((rows + 2 * ROWS, cols + LANES), F32),
            dma((members,)),
            dma((members,)),
            dma((ITERS, members)),
            dma((ITERS, members)),
            dma((ITERS, members)),
            dma((ITERS, members)),
            dma((ITERS, 2)),
            dma((ITERS, 2)),
            dma((ITERS, around)),
            dma((ITERS, around)),
        ],
        compiler_params=pltpu.CompilerParams(
            collective_id=0, has_side_effects=True, vmem_limit_bytes=48 * 1024 * 1024
        ),
    )(
        matrix_state,
        matrix_perm,
        frac_state.reshape(2, seg_rows, LANES),
        frac_aperture.reshape(seg_rows, LANES),
        link_cell[0, 0],
        link_seg[0, 0],
        link_trans[0, 0],
        link_count[0],
        link_upwind[:, 0, 0],
    )
    return matrix_out, frac_out.reshape(2, 1, segs)


def solution(mesh):
    return jax.shard_map(
        on_device,
        mesh=mesh,
        in_specs=(
            P(None, "grp", "frac"),
            P("grp", "frac"),
            P(None, "grp", "frac"),
            P("grp", "frac"),
            P("grp", "frac", None, None),
            P("grp", "frac", None, None),
            P("grp", "frac", None, None),
            P("grp", "frac", None),
            P(None, "grp", "frac", None, None),
        ),
        out_specs=(P(None, "grp", "frac"), P(None, "grp", "frac")),
        check_vma=False,
    )
```

```python
import functools

import jax
import jax.numpy as jnp
from jax import lax
from jax.experimental import pallas as pl
from jax.experimental.pallas import tpu as pltpu
from jax.sharding import PartitionSpec as P

ITERS = 3
SWEEPS = 4
LOW_BOUND = 0.02
HIGH_BOUND = 1.98
TAU_STEP = 0.5
MOBILITY_FLOOR = 0.2

F32 = jnp.float32
BF16 = jnp.bfloat16
MESH = pl.DeviceIdType.MESH
LANES = 128
ROWS = 8
AROUND = ((-1, 0), (1, 0), (0, -1), (0, 1), (-1, -1), (-1, 1), (1, -1), (1, 1))


def pieces(value):
    high = value.astype(BF16)
    low = (value - high.astype(F32)).astype(BF16)
    return high, low


def one_hot(index, count):
    ids = lax.broadcasted_iota(jnp.int32, (count, index.shape[1]), 0)
    return jnp.where(ids == index, F32(1.0), F32(0.0)).astype(BF16)


def spread(hot, values):
    rows, count = hot.shape
    stacked = hot.reshape(rows // 16, 16, count)
    out = []
    for value in values:
        for part in pieces(jnp.broadcast_to(value, (16, count))):
            out.append((stacked * part[None]).reshape(rows, count))
    return jnp.concatenate(out, axis=0)


def flux_terms(trans, upwind, cell_p, cell_s, seg_p, seg_s):
    u = jnp.where(upwind > 0.5, cell_s, seg_s)
    weight = trans * (MOBILITY_FLOOR + u * u)
    return weight, weight * (cell_p - seg_p) * u


def kernel(
    groups,
    members,
    cap,
    state_in,
    perm_in,
    frac_in,
    aperture_in,
    cell_in,
    seg_in,
    trans_in,
    count_in,
    upwind_in,
    matrix_out,
    frac_out,
    perm_ref,
    aperture_ref,
    cell_ref,
    seg_ref,
    trans_ref,
    count_ref,
    upwind_ref,
    stat_send,
    stat_recv,
    p_send,
    p_recv,
    f_send,
    f_recv,
    edge_left,
    edge_right,
    fields,
    sat,
    fq,
    side_send,
    halo_row,
    halo_col,
    col_hot,
    row_hot,
    low_hot,
    high_hot,
    cell_acc,
    seg_acc,
    ext_x,
    ext_inv,
    ext_c,
    stat_ss,
    stat_rs,
    p_ss,
    p_rs,
    f_ss,
    f_rs,
    edge_ss,
    edge_rs,
    halo_ss,
    halo_rs,
    load_sem,
):
    g = lax.axis_index("grp")
    me = lax.axis_index("frac")
    slots = members * cap
    rows, cols = perm_ref.shape
    seg_rows = aperture_ref.shape[0]
    group = min(slots, 4 * cap)

    def member(step):
        return lax.rem(me + step + members, members)

    def neighbour(step):
        return (lax.rem(g + step[0] + groups, groups), member(step[1]))

    loads = [
        pltpu.make_async_copy(src, dst, load_sem.at[i])
        for i, (src, dst) in enumerate(
            (
                (count_in, count_ref),
                (trans_in, trans_ref),
                (seg_in, seg_ref),
                (upwind_in, upwind_ref),
                (cell_in, cell_ref),
                (state_in.at[0], fields.at[0, 0]),
                (state_in.at[1], sat),
                (frac_in, fq.at[0]),
                (perm_in, perm_ref),
                (aperture_in, aperture_ref),
            )
        )
    ]
    for load in loads:
        load.start()

    barrier = pltpu.get_barrier_semaphore()
    for k in range(1, members):
        pl.semaphore_signal(barrier, inc=1, device_id=(g, member(k)), device_id_type=MESH)
    apart = [step for step in AROUND if step[0] != 0]
    for step in apart:
        pl.semaphore_signal(barrier, inc=1, device_id=neighbour(step), device_id_type=MESH)

    def lanes(block, width):
        return pl.ds(pl.multiple_of(block * width, width), width)

    for load in loads[:4]:
        load.wait()

    eye = lax.broadcasted_iota(jnp.int32, (members, members), 0) == lax.broadcasted_iota(
        jnp.int32, (members, members), 1
    )
    counts = jnp.sum(
        jnp.where(eye, jnp.broadcast_to(count_ref[...].astype(F32), (members, members)), 0.0),
        axis=1,
        keepdims=True,
    )
    place = lax.broadcasted_iota(jnp.int32, (members, cap), 1).astype(F32)
    live_trans = jnp.where(place < counts, trans_ref[...], F32(0.0))
    seg_float = seg_ref[...].astype(F32)
    ups = [upwind_ref[t].astype(F32) for t in range(ITERS)]
    stat_send[...] = jnp.zeros_like(stat_send)
    for o in range(members):
        here = slice(o * cap, (o + 1) * cap)
        stat_send[0:1, here] = live_trans[o : o + 1, :]
        stat_send[1:2, here] = seg_float[o : o + 1, :]
        for t in range(ITERS):
            stat_send[2 + t : 3 + t, here] = ups[t][o : o + 1, :]

    pl.semaphore_wait(barrier, members - 1 + len(apart))

    def exchange(send, recv, send_sem, recv_sem, k):
        to = member(k)
        return pltpu.make_async_remote_copy(
            src_ref=send.at[:, lanes(to, cap)],
            dst_ref=recv.at[:, lanes(me, cap)],
            send_sem=send_sem,
            recv_sem=recv_sem,
            device_id=(g, to),
            device_id_type=MESH,
        )

    def stat_copy(k):
        return exchange(stat_send, stat_recv, stat_ss.at[k], stat_rs.at[k], k)

    def p_copy(t, k):
        return exchange(p_send.at[t], p_recv.at[t], p_ss.at[t, k], p_rs.at[t, k], k)

    def f_copy(t, k):
        return exchange(f_send.at[t], f_recv.at[t], f_ss.at[t, k], f_rs.at[t, k], k)

    def each(body):
        lax.fori_loop(1, members, lambda k, c: (body(k), c)[1], 0)

    each(lambda k: stat_copy(k).start())
    stat_recv[:, lanes(me, cap)] = stat_send[:, lanes(me, cap)]

    def edge_copies(t):
        return (
            pltpu.make_async_remote_copy(
                src_ref=fq.at[t, 0, pl.ds(seg_rows - ROWS, ROWS), :],
                dst_ref=edge_left.at[t],
                send_sem=edge_ss.at[t, 0],
                recv_sem=edge_rs.at[t, 0],
                device_id=(g, member(1)),
                device_id_type=MESH,
            ),
            pltpu.make_async_remote_copy(
                src_ref=fq.at[t, 0, pl.ds(0, ROWS), :],
                dst_ref=edge_right.at[t],
                send_sem=edge_ss.at[t, 1],
                recv_sem=edge_rs.at[t, 1],
                device_id=(g, member(-1)),
                device_id_type=MESH,
            ),
        )

    def halo_copies(t):
        out = []
        for i, (dr, dc) in enumerate(AROUND):
            if dr == 0:
                src = side_send.at[t, i - 2]
                dst = halo_col.at[t, i - 2]
            else:
                edge = pl.ds(0 if dr < 0 else rows - ROWS, ROWS)
                if dc == 0:
                    src = fields.at[t, :, edge, :]
                    dst = halo_row.at[t, i]
                else:
                    src = fields.at[t, :, edge, pl.ds(0 if dc < 0 else cols - LANES, LANES)]
                    dst = halo_col.at[t, i - 2]
            out.append(
                pltpu.make_async_remote_copy(
                    src_ref=src,
                    dst_ref=dst,
                    send_sem=halo_ss.at[t, i],
                    recv_sem=halo_rs.at[t, i],
                    device_id=neighbour((dr, dc)),
                    device_id_type=MESH,
                )
            )
        return out

    for load in loads[4:]:
        load.wait()

    def cell_hots(o, carry):
        index = cell_ref[pl.ds(o, 1), :]
        col_hot[:, lanes(o, cap)] = one_hot(lax.rem(index, cols), cols)
        row_hot[:, lanes(o, cap)] = one_hot(lax.div(index, cols), rows)
        return carry

    lax.fori_loop(0, members, cell_hots, 0)

    each(lambda k: stat_copy(k).wait_recv())

    def seg_hots(o, carry):
        index = stat_recv[1:2, lanes(o, cap)].astype(jnp.int32)
        low_hot[:, lanes(o, cap)] = one_hot(lax.rem(index, LANES), LANES)
        high_hot[:, lanes(o, cap)] = one_hot(lax.div(index, LANES), seg_rows)
        return carry

    lax.fori_loop(0, members, seg_hots, 0)

    def gather(per, table, hot_cols, hot_rows, add, send, recv, copy, t):
        height = hot_rows.shape[0]

        def body(j, carry):
            q = lax.rem(lax.div(me, per) + j, members // per)
            here = lanes(q, per * cap)
            picked = add(jnp.dot(table, hot_cols(here), preferred_element_type=F32))
            hot = hot_rows[:, here].astype(F32)
            for f in range(2):
                send[t, f : f + 1, here] = jnp.sum(
                    picked[f * height : (f + 1) * height] * hot, axis=0, keepdims=True
                )
            for i in range(per):
                k = lax.rem(q * per + i - me + members, members)

                @pl.when(k > 0)
                def _():
                    copy(t, k).start()

            return carry

        lax.fori_loop(0, members // per, body, 0)
        recv[t, :, lanes(me, cap)] = send[t, :, lanes(me, cap)]

    def gather_segments(t):
        for copy in edge_copies(t):
            copy.start()
        table = jnp.concatenate(
            [jnp.concatenate(pieces(fq[t, f]), axis=1) for f in range(2)], axis=0
        )

        def both(here):
            low = low_hot[:, here]
            return jnp.concatenate([low, low], axis=0)

        gather(min(members, 16), table, both, high_hot, lambda x: x, f_send, f_recv, f_copy, t)

    def gather_cells(t):
        highs, lows = zip(pieces(fields[t, 0]), pieces(sat[...]))
        table = jnp.concatenate(highs + lows, axis=0)
        gather(
            min(members, 4),
            table,
            lambda here: col_hot[:, here],
            row_hot,
            lambda x: x[: 2 * rows] + x[2 * rows :],
            p_send,
            p_recv,
            p_copy,
            t,
        )

    def collect(acc, hot_rows, hot_cols, values_of):
        acc[...] = jnp.zeros_like(acc)

        def body(j, carry):
            here = lanes(j, group)
            left = spread(hot_rows[:, here], values_of(here))
            acc[...] += lax.dot_general(
                left, hot_cols[:, here], (((1,), (1,)), ((), ())), preferred_element_type=F32
            )
            return carry

        lax.fori_loop(0, slots // group, body, 0)
        height = hot_rows.shape[0]
        return [
            acc[2 * f * height : (2 * f + 1) * height]
            + acc[(2 * f + 1) * height : (2 * f + 2) * height]
            for f in range(3)
        ]

    def scatter_cells(t):
        def values_of(here):
            seg_p = f_recv[t, 0:1, here]
            weight, water = flux_terms(
                stat_send[0:1, here],
                stat_send[pl.ds(2 + t, 1), here],
                p_send[t, 0:1, here],
                p_send[t, 1:2, here],
                seg_p,
                f_recv[t, 1:2, here],
            )
            return weight, weight * seg_p, water

        couple, source, lost = collect(cell_acc, row_hot, col_hot, values_of)
        perm = perm_ref[...]
        p = fields[t, 0]
        inverse = 1.0 / (4.0 + perm + couple)
        scaled = inverse * (perm * p + source)
        sat[...] = sat[...] - TAU_STEP * lost / (perm + couple)
        fields[t, 1] = inverse
        fields[t, 2] = scaled
        for f, field in enumerate((p, inverse, scaled)):
            side_send[t, 0, f] = jnp.transpose(field[:, :LANES])[:ROWS]
            side_send[t, 1, f] = jnp.transpose(field[:, cols - LANES :])[LANES - ROWS :]

    def scatter_segments(t):
        def values_of(here):
            cell_p = p_recv[t, 0:1, here]
            weight, water = flux_terms(
                stat_recv[0:1, here],
                stat_recv[pl.ds(2 + t, 1), here],
                cell_p,
                p_recv[t, 1:2, here],
                f_send[t, 0:1, here],
                f_send[t, 1:2, here],
            )
            return weight * cell_p, weight, water

        inflow, total, gained = collect(seg_acc, high_hot, low_hot, values_of)
        for copy in edge_copies(t):
            copy.wait_recv()
        aperture = aperture_ref[...]
        p = fq[t, 0]
        first = jnp.where(me > 0, edge_left[t, ROWS - 1 : ROWS, LANES - 1 : LANES], F32(0.0))
        last = jnp.where(me < members - 1, edge_right[t, 0:1, 0:1], F32(0.0))
        lane = lax.broadcasted_iota(jnp.int32, (seg_rows, LANES), 1)
        row = lax.broadcasted_iota(jnp.int32, (seg_rows, LANES), 0)
        turned = pltpu.roll(p, 1, axis=1)
        left = jnp.where(lane == 0, pltpu.roll(turned, 1, axis=0), turned)
        left = jnp.where((lane == 0) & (row == 0), first, left)
        turned = pltpu.roll(p, LANES - 1, axis=1)
        right = jnp.where(lane == LANES - 1, pltpu.roll(turned, seg_rows - 1, axis=0), turned)
        right = jnp.where((lane == LANES - 1) & (row == seg_rows - 1), last, right)
        fq[t + 1, 0] = (aperture * p + inflow + left + right) / (aperture + total + 2.0)
        fq[t + 1, 1] = fq[t, 1] + TAU_STEP * gained / (aperture + total)

    def sweeps(t):
        for copy in halo_copies(t):
            copy.wait_recv()
        inside = {
            -1: jnp.where(g > 0, F32(1.0), F32(0.0)),
            1: jnp.where(g < groups - 1, F32(1.0), F32(0.0)),
            0: F32(1.0),
        }
        beside = {
            -1: jnp.where(me > 0, F32(1.0), F32(0.0)),
            1: jnp.where(me < members - 1, F32(1.0), F32(0.0)),
        }
        corner = {
            (-dr, -dc): i - 2 for i, (dr, dc) in enumerate(AROUND) if dc != 0
        }
        east = lax.broadcasted_iota(jnp.int32, (ROWS, LANES), 1) < LANES // 2
        filler = jnp.zeros((LANES - 2 * ROWS, LANES), F32)
        for f, ext in enumerate((ext_x, ext_inv, ext_c)):
            ext[0:ROWS, 0:cols] = halo_row[t, 1, f] * inside[-1]
            ext[ROWS : ROWS + rows, 0:cols] = fields[t, f]
            ext[ROWS + rows :, 0:cols] = halo_row[t, 0, f] * inside[1]
            for dr, at in ((-1, slice(0, ROWS)), (1, slice(ROWS + rows, rows + 2 * ROWS))):
                ext[at, cols:] = jnp.where(
                    east,
                    halo_col[t, corner[dr, 1], f] * (inside[dr] * beside[1]),
                    halo_col[t, corner[dr, -1], f] * (inside[dr] * beside[-1]),
                )
            ext[ROWS : ROWS + rows, cols:] = jnp.transpose(
                jnp.concatenate(
                    [
                        halo_col[t, corner[0, 1], f] * beside[1],
                        filler,
                        halo_col[t, corner[0, -1], f] * beside[-1],
                    ],
                    axis=0,
                )
            )

        height, width = ext_x.shape
        inverse = ext_inv[...]
        scaled = ext_c[...]

        def residual_of(x):
            around = (
                pltpu.roll(x, 1, axis=0)
                + pltpu.roll(x, height - 1, axis=0)
                + pltpu.roll(x, 1, axis=1)
                + pltpu.roll(x, width - 1, axis=1)
            )
            return inverse * around + (scaled - x)

        centre = 0.5 * (HIGH_BOUND + LOW_BOUND)
        half_width = 0.5 * (HIGH_BOUND - LOW_BOUND)
        scale_ratio = centre / half_width
        ratio_now = 1.0 / scale_ratio
        x = ext_x[...]
        update = residual_of(x) / centre
        for sweep_index in range(SWEEPS):
            x = x + update
            if sweep_index + 1 < SWEEPS:
                ratio_next = 1.0 / (2.0 * scale_ratio - ratio_now)
                update = ratio_next * ratio_now * update + (
                    2.0 * ratio_next / half_width
                ) * residual_of(x)
                ratio_now = ratio_next
        fields[t + 1, 0] = x[ROWS : ROWS + rows, :cols]

    gather_segments(0)

    def outer(t, carry):
        gather_cells(t)
        each(lambda k: f_copy(t, k).wait_recv())
        scatter_cells(t)
        for copy in halo_copies(t):
            copy.start()
        each(lambda k: p_copy(t, k).wait_recv())
        scatter_segments(t)

        @pl.when(t + 1 < ITERS)
        def _():
            gather_segments(t + 1)

        sweeps(t)
        return carry

    lax.fori_loop(0, ITERS, outer, 0)

    matrix_out[0] = fields[ITERS, 0]
    matrix_out[1] = sat[...]
    frac_out[...] = fq[ITERS]

    each(lambda k: stat_copy(k).wait_send())

    def drain(t, carry):
        each(lambda k: p_copy(t, k).wait_send())
        each(lambda k: f_copy(t, k).wait_send())
        for copy in edge_copies(t):
            copy.wait_send()
        for copy in halo_copies(t):
            copy.wait_send()
        return carry

    lax.fori_loop(0, ITERS, drain, 0)


def write_out(matrix_in, frac_in, matrix_out, frac_out, sems):
    copies = (
        pltpu.make_async_copy(matrix_in, matrix_out, sems.at[0]),
        pltpu.make_async_copy(frac_in, frac_out, sems.at[1]),
    )
    for copy in copies:
        copy.start()
    for copy in copies:
        copy.wait()


def on_device(
    matrix_state,
    matrix_perm,
    frac_state,
    frac_aperture,
    link_cell,
    link_seg,
    link_trans,
    link_count,
    link_upwind,
):
    groups = lax.axis_size("grp")
    members, cap = link_cell.shape[2:]
    rows, cols = matrix_perm.shape
    segs = frac_aperture.shape[1]
    seg_rows = segs // LANES
    slots = members * cap
    vmem = pl.BlockSpec(memory_space=pltpu.VMEM)
    hbm = pl.BlockSpec(memory_space=pltpu.HBM)
    dma = pltpu.SemaphoreType.DMA
    around = len(AROUND)
    matrix_out, frac_out = pl.pallas_call(
        functools.partial(kernel, groups, members, cap),
        out_shape=(
            jax.ShapeDtypeStruct(matrix_state.shape, F32),
            jax.ShapeDtypeStruct((2, seg_rows, LANES), F32),
        ),
        in_specs=[hbm] * 9,
        out_specs=(vmem, vmem),
        scratch_shapes=[
            pltpu.VMEM((rows, cols), F32),
            pltpu.VMEM((seg_rows, LANES), F32),
            pltpu.VMEM((members, cap), jnp.int32),
            pltpu.VMEM((members, cap), jnp.int32),
            pltpu.VMEM((members, cap), F32),
            pltpu.VMEM((1, members), jnp.int32),
            pltpu.VMEM((ITERS, members, cap), jnp.int32),
            pltpu.VMEM((ROWS, slots), F32),
            pltpu.VMEM((ROWS, slots), F32),
            pltpu.VMEM((ITERS, 2, slots), F32),
            pltpu.VMEM((ITERS, 2, slots), F32),
            pltpu.VMEM((ITERS, 2, slots), F32),
            pltpu.VMEM((ITERS, 2, slots), F32),
            pltpu.VMEM((ITERS, ROWS, LANES), F32),
            pltpu.VMEM((ITERS, ROWS, LANES), F32),
            pltpu.VMEM((ITERS + 1, 3, rows, cols), F32),
            pltpu.VMEM((rows, cols), F32),
            pltpu.VMEM((ITERS + 1, 2, seg_rows, LANES), F32),
            pltpu.VMEM((ITERS, 2, 3, ROWS, LANES), F32),
            pltpu.VMEM((ITERS, 2, 3, ROWS, cols), F32),
            pltpu.VMEM((ITERS, 6, 3, ROWS, LANES), F32),
            pltpu.VMEM((cols, slots), BF16),
            pltpu.VMEM((rows, slots), BF16),
            pltpu.VMEM((LANES, slots), BF16),
            pltpu.VMEM((seg_rows, slots), BF16),
            pltpu.VMEM((6 * rows, cols), F32),
            pltpu.VMEM((6 * seg_rows, LANES), F32),
            pltpu.VMEM((rows + 2 * ROWS, cols + LANES), F32),
            pltpu.VMEM((rows + 2 * ROWS, cols + LANES), F32),
            pltpu.VMEM((rows + 2 * ROWS, cols + LANES), F32),
            dma((members,)),
            dma((members,)),
            dma((ITERS, members)),
            dma((ITERS, members)),
            dma((ITERS, members)),
            dma((ITERS, members)),
            dma((ITERS, 2)),
            dma((ITERS, 2)),
            dma((ITERS, around)),
            dma((ITERS, around)),
            dma((10,)),
        ],
        compiler_params=pltpu.CompilerParams(
            collective_id=0, has_side_effects=True, vmem_limit_bytes=40 * 1024 * 1024
        ),
    )(
        *(
            pltpu.with_memory_space_constraint(x, pltpu.HBM)
            for x in (
                matrix_state,
                matrix_perm,
                frac_state.reshape(2, seg_rows, LANES),
                frac_aperture.reshape(seg_rows, LANES),
                link_cell[0, 0],
                link_seg[0, 0],
                link_trans[0, 0],
                link_count[0],
                link_upwind[:, 0, 0],
            )
        )
    )
    matrix_out, frac_out = pl.pallas_call(
        write_out,
        out_shape=(
            jax.ShapeDtypeStruct(matrix_state.shape, F32),
            jax.ShapeDtypeStruct((2, seg_rows, LANES), F32),
        ),
        in_specs=[vmem] * 2,
        out_specs=(hbm, hbm),
        scratch_shapes=[dma((2,))],
        compiler_params=pltpu.CompilerParams(vmem_limit_bytes=4 * 1024 * 1024),
    )(matrix_out, frac_out)
    return matrix_out, frac_out.reshape(2, 1, segs)


def solution(mesh):
    return jax.shard_map(
        on_device,
        mesh=mesh,
        in_specs=(
            P(None, "grp", "frac"),
            P("grp", "frac"),
            P(None, "grp", "frac"),
            P("grp", "frac"),
            P("grp", "frac", None, None),
            P("grp", "frac", None, None),
            P("grp", "frac", None, None),
            P("grp", "frac", None),
            P(None, "grp", "frac", None, None),
        ),
        out_specs=(P(None, "grp", "frac"), P(None, "grp", "frac")),
        check_vma=False,
    )
```

```python
import functools

import jax
import jax.numpy as jnp
from jax import lax
from jax.experimental import pallas as pl
from jax.experimental.pallas import tpu as pltpu
from jax.sharding import PartitionSpec as P

ITERS = 3
SWEEPS = 4
LOW_BOUND = 0.02
HIGH_BOUND = 1.98
TAU_STEP = 0.5
MOBILITY_FLOOR = 0.2

F32 = jnp.float32
BF16 = jnp.bfloat16
MESH = pl.DeviceIdType.MESH
LANES = 128
ROWS = 8
AROUND = ((-1, 0), (1, 0), (0, -1), (0, 1), (-1, -1), (-1, 1), (1, -1), (1, 1))


def pieces(value):
    high = value.astype(BF16)
    low = (value - high.astype(F32)).astype(BF16)
    return high, low


def one_hot(index, count):
    ids = lax.broadcasted_iota(jnp.int32, (count, index.shape[1]), 0)
    return jnp.where(ids == index, F32(1.0), F32(0.0)).astype(BF16)


def spread(hot, values):
    rows, count = hot.shape
    stacked = hot.reshape(rows // 16, 16, count)
    out = []
    for value in values:
        for part in pieces(jnp.broadcast_to(value, (16, count))):
            out.append((stacked * part[None]).reshape(rows, count))
    return jnp.concatenate(out, axis=0)


def flux_terms(trans, upwind, cell_p, cell_s, seg_p, seg_s):
    u = jnp.where(upwind > 0.5, cell_s, seg_s)
    weight = trans * (MOBILITY_FLOOR + u * u)
    return weight, weight * (cell_p - seg_p) * u


def kernel(
    groups,
    members,
    cap,
    state_in,
    perm_in,
    frac_in,
    aperture_in,
    cell_in,
    seg_in,
    trans_in,
    count_in,
    upwind_in,
    matrix_out,
    frac_out,
    perm_ref,
    aperture_ref,
    cell_ref,
    seg_ref,
    trans_ref,
    count_ref,
    upwind_ref,
    stat_send,
    stat_recv,
    p_send,
    p_recv,
    f_send,
    f_recv,
    edges,
    fields,
    sat,
    fq,
    side_send,
    halo_row,
    halo_col,
    col_hot,
    row_hot,
    low_hot,
    high_hot,
    cell_acc,
    seg_acc,
    ext_x,
    ext_inv,
    ext_c,
    stat_ss,
    stat_rs,
    p_ss,
    p_rs,
    f_ss,
    f_rs,
    edge_ss,
    edge_rs,
    halo_ss,
    halo_rs,
    load_sem,
):
    g = lax.axis_index("grp")
    me = lax.axis_index("frac")
    slots = members * cap
    rows, cols = perm_ref.shape
    seg_rows = aperture_ref.shape[0]
    group = min(slots, 4 * cap)

    def member(step):
        return lax.rem(me + step + members, members)

    def neighbour(step):
        return (lax.rem(g + step[0] + groups, groups), member(step[1]))

    loads = [
        pltpu.make_async_copy(src, dst, load_sem.at[i])
        for i, (src, dst) in enumerate(
            (
                (count_in, count_ref),
                (trans_in, trans_ref),
                (seg_in, seg_ref),
                (upwind_in, upwind_ref),
                (cell_in, cell_ref),
                (state_in.at[0], fields.at[0, 0]),
                (state_in.at[1], sat),
                (frac_in, fq.at[0]),
                (perm_in, perm_ref),
                (aperture_in, aperture_ref),
            )
        )
    ]
    for load in loads:
        load.start()

    barrier = pltpu.get_barrier_semaphore()
    for k in range(1, members):
        pl.semaphore_signal(barrier, inc=1, device_id=(g, member(k)), device_id_type=MESH)
    apart = [step for step in AROUND if step[0] != 0]
    for step in apart:
        pl.semaphore_signal(barrier, inc=1, device_id=neighbour(step), device_id_type=MESH)

    def lanes(block, width):
        return pl.ds(pl.multiple_of(block * width, width), width)

    for load in loads[:4]:
        load.wait()

    eye = lax.broadcasted_iota(jnp.int32, (members, members), 0) == lax.broadcasted_iota(
        jnp.int32, (members, members), 1
    )
    counts = jnp.sum(
        jnp.where(eye, jnp.broadcast_to(count_ref[...].astype(F32), (members, members)), 0.0),
        axis=1,
        keepdims=True,
    )
    place = lax.broadcasted_iota(jnp.int32, (members, cap), 1).astype(F32)
    live_trans = jnp.where(place < counts, trans_ref[...], F32(0.0))
    seg_float = seg_ref[...].astype(F32)
    ups = [upwind_ref[t].astype(F32) for t in range(ITERS)]
    stat_send[...] = jnp.zeros_like(stat_send)
    for o in range(members):
        here = slice(o * cap, (o + 1) * cap)
        stat_send[0:1, here] = live_trans[o : o + 1, :]
        stat_send[1:2, here] = seg_float[o : o + 1, :]
        for t in range(ITERS):
            stat_send[2 + t : 3 + t, here] = ups[t][o : o + 1, :]

    pl.semaphore_wait(barrier, members - 1 + len(apart))

    def exchange(send, recv, send_sem, recv_sem, k):
        to = member(k)
        return pltpu.make_async_remote_copy(
            src_ref=send.at[:, lanes(to, cap)],
            dst_ref=recv.at[:, lanes(me, cap)],
            send_sem=send_sem,
            recv_sem=recv_sem,
            device_id=(g, to),
            device_id_type=MESH,
        )

    def stat_copy(k):
        return exchange(stat_send, stat_recv, stat_ss, stat_rs, k)

    def p_copy(t, k):
        return exchange(p_send.at[t], p_recv.at[t], p_ss.at[t], p_rs.at[t], k)

    def f_copy(t, k):
        return exchange(f_send.at[t], f_recv.at[t], f_ss.at[t], f_rs.at[t], k)

    def total(ref, send_sem, recv_sem):
        return pltpu.make_async_remote_copy(
            src_ref=ref,
            dst_ref=ref,
            send_sem=send_sem,
            recv_sem=recv_sem,
            device_id=(g, member(1)),
            device_id_type=MESH,
        )

    others = slots - cap

    def stat_all():
        return total(stat_recv.at[:, :others], stat_ss, stat_rs)

    def p_all(t):
        return total(p_recv.at[t, :, :others], p_ss.at[t], p_rs.at[t])

    def f_all(t):
        return total(f_recv.at[t, :, :others], f_ss.at[t], f_rs.at[t])

    def edge_all(t):
        return total(edges.at[t], edge_ss.at[t], edge_rs.at[t])

    def halo_all(t):
        return (
            total(halo_row.at[t], halo_ss.at[t, 0], halo_rs.at[t, 0]),
            total(halo_col.at[t], halo_ss.at[t, 1], halo_rs.at[t, 1]),
        )

    def each(body):
        lax.fori_loop(1, members, lambda k, c: (body(k), c)[1], 0)

    each(lambda k: stat_copy(k).start())
    stat_recv[:, lanes(me, cap)] = stat_send[:, lanes(me, cap)]

    def edge_copies(t):
        return (
            pltpu.make_async_remote_copy(
                src_ref=fq.at[t, 0, pl.ds(seg_rows - ROWS, ROWS), :],
                dst_ref=edges.at[t, 0],
                send_sem=edge_ss.at[t],
                recv_sem=edge_rs.at[t],
                device_id=(g, member(1)),
                device_id_type=MESH,
            ),
            pltpu.make_async_remote_copy(
                src_ref=fq.at[t, 0, pl.ds(0, ROWS), :],
                dst_ref=edges.at[t, 1],
                send_sem=edge_ss.at[t],
                recv_sem=edge_rs.at[t],
                device_id=(g, member(-1)),
                device_id_type=MESH,
            ),
        )

    def halo_copies(t):
        out = []
        for i, (dr, dc) in enumerate(AROUND):
            kind = 0 if dc == 0 else 1
            if dr == 0:
                src = side_send.at[t, i - 2]
                dst = halo_col.at[t, i - 2]
            else:
                edge = pl.ds(0 if dr < 0 else rows - ROWS, ROWS)
                if dc == 0:
                    src = fields.at[t, :, edge, :]
                    dst = halo_row.at[t, i]
                else:
                    src = fields.at[t, :, edge, pl.ds(0 if dc < 0 else cols - LANES, LANES)]
                    dst = halo_col.at[t, i - 2]
            out.append(
                pltpu.make_async_remote_copy(
                    src_ref=src,
                    dst_ref=dst,
                    send_sem=halo_ss.at[t, kind],
                    recv_sem=halo_rs.at[t, kind],
                    device_id=neighbour((dr, dc)),
                    device_id_type=MESH,
                )
            )
        return out

    for load in loads[4:]:
        load.wait()

    def cell_hots(o, carry):
        index = cell_ref[pl.ds(o, 1), :]
        col_hot[:, lanes(o, cap)] = one_hot(lax.rem(index, cols), cols)
        row_hot[:, lanes(o, cap)] = one_hot(lax.div(index, cols), rows)
        return carry

    lax.fori_loop(0, members, cell_hots, 0)

    stat_all().wait_recv()

    def seg_hots(o, carry):
        index = stat_recv[1:2, lanes(o, cap)].astype(jnp.int32)
        low_hot[:, lanes(o, cap)] = one_hot(lax.rem(index, LANES), LANES)
        high_hot[:, lanes(o, cap)] = one_hot(lax.div(index, LANES), seg_rows)
        return carry

    lax.fori_loop(0, members, seg_hots, 0)

    def gather(per, table, hot_cols, hot_rows, add, send, recv, copy, t):
        height = hot_rows.shape[0]

        def body(j, carry):
            q = lax.rem(lax.div(me, per) + j, members // per)
            here = lanes(q, per * cap)
            picked = add(jnp.dot(table, hot_cols(here), preferred_element_type=F32))
            hot = hot_rows[:, here].astype(F32)
            for f in range(2):
                send[t, f : f + 1, here] = jnp.sum(
                    picked[f * height : (f + 1) * height] * hot, axis=0, keepdims=True
                )
            for i in range(per):
                k = lax.rem(q * per + i - me + members, members)

                @pl.when(k > 0)
                def _():
                    copy(t, k).start()

            return carry

        lax.fori_loop(0, members // per, body, 0)
        recv[t, :, lanes(me, cap)] = send[t, :, lanes(me, cap)]

    def gather_segments(t):
        for copy in edge_copies(t):
            copy.start()
        table = jnp.concatenate(
            [jnp.concatenate(pieces(fq[t, f]), axis=1) for f in range(2)], axis=0
        )

        def both(here):
            low = low_hot[:, here]
            return jnp.concatenate([low, low], axis=0)

        gather(min(members, 16), table, both, high_hot, lambda x: x, f_send, f_recv, f_copy, t)

    def gather_cells(t):
        highs, lows = zip(pieces(fields[t, 0]), pieces(sat[...]))
        table = jnp.concatenate(highs + lows, axis=0)
        gather(
            min(members, 4),
            table,
            lambda here: col_hot[:, here],
            row_hot,
            lambda x: x[: 2 * rows] + x[2 * rows :],
            p_send,
            p_recv,
            p_copy,
            t,
        )

    def collect(group, acc, hot_rows, hot_cols, values_of):
        acc[...] = jnp.zeros_like(acc)

        def body(j, carry):
            here = lanes(j, group)
            left = spread(hot_rows[:, here], values_of(here))
            acc[...] += lax.dot_general(
                left, hot_cols[:, here], (((1,), (1,)), ((), ())), preferred_element_type=F32
            )
            return carry

        lax.fori_loop(0, slots // group, body, 0)
        height = hot_rows.shape[0]
        return [
            acc[2 * f * height : (2 * f + 1) * height]
            + acc[(2 * f + 1) * height : (2 * f + 2) * height]
            for f in range(3)
        ]

    def scatter_cells(t):
        def values_of(here):
            seg_p = f_recv[t, 0:1, here]
            weight, water = flux_terms(
                stat_send[0:1, here],
                stat_send[pl.ds(2 + t, 1), here],
                p_send[t, 0:1, here],
                p_send[t, 1:2, here],
                seg_p,
                f_recv[t, 1:2, here],
            )
            return weight, weight * seg_p, water

        couple, source, lost = collect(min(slots, 2048), cell_acc, row_hot, col_hot, values_of)
        perm = perm_ref[...]
        p = fields[t, 0]
        inverse = 1.0 / (4.0 + perm + couple)
        scaled = inverse * (perm * p + source)
        sat[...] = sat[...] - TAU_STEP * lost / (perm + couple)
        fields[t, 1] = inverse
        fields[t, 2] = scaled
        for f, field in enumerate((p, inverse, scaled)):
            side_send[t, 0, f] = jnp.transpose(field[:, :LANES])[:ROWS]
            side_send[t, 1, f] = jnp.transpose(field[:, cols - LANES :])[LANES - ROWS :]

    def scatter_segments(t):
        def values_of(here):
            cell_p = p_recv[t, 0:1, here]
            weight, water = flux_terms(
                stat_recv[0:1, here],
                stat_recv[pl.ds(2 + t, 1), here],
                cell_p,
                p_recv[t, 1:2, here],
                f_send[t, 0:1, here],
                f_send[t, 1:2, here],
            )
            return weight * cell_p, weight, water

        inflow, conduct, gained = collect(min(slots, 4096), seg_acc, high_hot, low_hot, values_of)
        edge_all(t).wait_recv()
        aperture = aperture_ref[...]
        p = fq[t, 0]
        first = jnp.where(me > 0, edges[t, 0, ROWS - 1 : ROWS, LANES - 1 : LANES], F32(0.0))
        last = jnp.where(me < members - 1, edges[t, 1, 0:1, 0:1], F32(0.0))
        lane = lax.broadcasted_iota(jnp.int32, (seg_rows, LANES), 1)
        row = lax.broadcasted_iota(jnp.int32, (seg_rows, LANES), 0)
        turned = pltpu.roll(p, 1, axis=1)
        left = jnp.where(lane == 0, pltpu.roll(turned, 1, axis=0), turned)
        left = jnp.where((lane == 0) & (row == 0), first, left)
        turned = pltpu.roll(p, LANES - 1, axis=1)
        right = jnp.where(lane == LANES - 1, pltpu.roll(turned, seg_rows - 1, axis=0), turned)
        right = jnp.where((lane == LANES - 1) & (row == seg_rows - 1), last, right)
        fq[t + 1, 0] = (aperture * p + inflow + left + right) / (aperture + conduct + 2.0)
        fq[t + 1, 1] = fq[t, 1] + TAU_STEP * gained / (aperture + conduct)

    def sweeps(t):
        for copy in halo_all(t):
            copy.wait_recv()
        inside = {
            -1: jnp.where(g > 0, F32(1.0), F32(0.0)),
            1: jnp.where(g < groups - 1, F32(1.0), F32(0.0)),
            0: F32(1.0),
        }
        beside = {
            -1: jnp.where(me > 0, F32(1.0), F32(0.0)),
            1: jnp.where(me < members - 1, F32(1.0), F32(0.0)),
        }
        corner = {
            (-dr, -dc): i - 2 for i, (dr, dc) in enumerate(AROUND) if dc != 0
        }
        east = lax.broadcasted_iota(jnp.int32, (ROWS, LANES), 1) < LANES // 2
        filler = jnp.zeros((LANES - 2 * ROWS, LANES), F32)
        for f, ext in enumerate((ext_x, ext_inv, ext_c)):
            ext[0:ROWS, 0:cols] = halo_row[t, 1, f] * inside[-1]
            ext[ROWS : ROWS + rows, 0:cols] = fields[t, f]
            ext[ROWS + rows :, 0:cols] = halo_row[t, 0, f] * inside[1]
            for dr, at in ((-1, slice(0, ROWS)), (1, slice(ROWS + rows, rows + 2 * ROWS))):
                ext[at, cols:] = jnp.where(
                    east,
                    halo_col[t, corner[dr, 1], f] * (inside[dr] * beside[1]),
                    halo_col[t, corner[dr, -1], f] * (inside[dr] * beside[-1]),
                )
            ext[ROWS : ROWS + rows, cols:] = jnp.transpose(
                jnp.concatenate(
                    [
                        halo_col[t, corner[0, 1], f] * beside[1],
                        filler,
                        halo_col[t, corner[0, -1], f] * beside[-1],
                    ],
                    axis=0,
                )
            )

        height, width = ext_x.shape
        inverse = ext_inv[...]
        scaled = ext_c[...]

        def residual_of(x):
            around = (
                pltpu.roll(x, 1, axis=0)
                + pltpu.roll(x, height - 1, axis=0)
                + pltpu.roll(x, 1, axis=1)
                + pltpu.roll(x, width - 1, axis=1)
            )
            return inverse * around + (scaled - x)

        centre = 0.5 * (HIGH_BOUND + LOW_BOUND)
        half_width = 0.5 * (HIGH_BOUND - LOW_BOUND)
        scale_ratio = centre / half_width
        ratio_now = 1.0 / scale_ratio
        x = ext_x[...]
        update = residual_of(x) / centre
        for sweep_index in range(SWEEPS):
            x = x + update
            if sweep_index + 1 < SWEEPS:
                ratio_next = 1.0 / (2.0 * scale_ratio - ratio_now)
                update = ratio_next * ratio_now * update + (
                    2.0 * ratio_next / half_width
                ) * residual_of(x)
                ratio_now = ratio_next
        fields[t + 1, 0] = x[ROWS : ROWS + rows, :cols]

    gather_segments(0)

    def outer(t, carry):
        gather_cells(t)
        f_all(t).wait_recv()
        scatter_cells(t)
        for copy in halo_copies(t):
            copy.start()
        p_all(t).wait_recv()
        scatter_segments(t)

        @pl.when(t + 1 < ITERS)
        def _():
            gather_segments(t + 1)

        sweeps(t)
        return carry

    lax.fori_loop(0, ITERS, outer, 0)

    matrix_out[0] = fields[ITERS, 0]
    matrix_out[1] = sat[...]
    frac_out[...] = fq[ITERS]

    stat_all().wait_send()

    def drain(t, carry):
        for copy in (p_all(t), f_all(t), edge_all(t), *halo_all(t)):
            copy.wait_send()
        return carry

    lax.fori_loop(0, ITERS, drain, 0)


def write_out(matrix_in, frac_in, matrix_out, frac_out, sems):
    copies = (
        pltpu.make_async_copy(matrix_in, matrix_out, sems.at[0]),
        pltpu.make_async_copy(frac_in, frac_out, sems.at[1]),
    )
    for copy in copies:
        copy.start()
    for copy in copies:
        copy.wait()


def on_device(
    matrix_state,
    matrix_perm,
    frac_state,
    frac_aperture,
    link_cell,
    link_seg,
    link_trans,
    link_count,
    link_upwind,
):
    groups = lax.axis_size("grp")
    members, cap = link_cell.shape[2:]
    rows, cols = matrix_perm.shape
    segs = frac_aperture.shape[1]
    seg_rows = segs // LANES
    slots = members * cap
    vmem = pl.BlockSpec(memory_space=pltpu.VMEM)
    hbm = pl.BlockSpec(memory_space=pltpu.HBM)
    dma = pltpu.SemaphoreType.DMA
    around = len(AROUND)
    matrix_out, frac_out = pl.pallas_call(
        functools.partial(kernel, groups, members, cap),
        out_shape=(
            jax.ShapeDtypeStruct(matrix_state.shape, F32),
            jax.ShapeDtypeStruct((2, seg_rows, LANES), F32),
        ),
        in_specs=[hbm] * 9,
        out_specs=(vmem, vmem),
        scratch_shapes=[
            pltpu.VMEM((rows, cols), F32),
            pltpu.VMEM((seg_rows, LANES), F32),
            pltpu.VMEM((members, cap), jnp.int32),
            pltpu.VMEM((members, cap), jnp.int32),
            pltpu.VMEM((members, cap), F32),
            pltpu.VMEM((1, members), jnp.int32),
            pltpu.VMEM((ITERS, members, cap), jnp.int32),
            pltpu.VMEM((ROWS, slots), F32),
            pltpu.VMEM((ROWS, slots), F32),
            pltpu.VMEM((ITERS, 2, slots), F32),
            pltpu.VMEM((ITERS, 2, slots), F32),
            pltpu.VMEM((ITERS, 2, slots), F32),
            pltpu.VMEM((ITERS, 2, slots), F32),
            pltpu.VMEM((ITERS, 2, ROWS, LANES), F32),
            pltpu.VMEM((ITERS + 1, 3, rows, cols), F32),
            pltpu.VMEM((rows, cols), F32),
            pltpu.VMEM((ITERS + 1, 2, seg_rows, LANES), F32),
            pltpu.VMEM((ITERS, 2, 3, ROWS, LANES), F32),
            pltpu.VMEM((ITERS, 2, 3, ROWS, cols), F32),
            pltpu.VMEM((ITERS, 6, 3, ROWS, LANES), F32),
            pltpu.VMEM((cols, slots), BF16),
            pltpu.VMEM((rows, slots), BF16),
            pltpu.VMEM((LANES, slots), BF16),
            pltpu.VMEM((seg_rows, slots), BF16),
            pltpu.VMEM((6 * rows, cols), F32),
            pltpu.VMEM((6 * seg_rows, LANES), F32),
            pltpu.VMEM((rows + 2 * ROWS, cols + LANES), F32),
            pltpu.VMEM((rows + 2 * ROWS, cols + LANES), F32),
            pltpu.VMEM((rows + 2 * ROWS, cols + LANES), F32),
            dma(()),
            dma(()),
            dma((ITERS,)),
            dma((ITERS,)),
            dma((ITERS,)),
            dma((ITERS,)),
            dma((ITERS,)),
            dma((ITERS,)),
            dma((ITERS, 2)),
            dma((ITERS, 2)),
            dma((10,)),
        ],
        compiler_params=pltpu.CompilerParams(
            collective_id=0, has_side_effects=True, vmem_limit_bytes=40 * 1024 * 1024
        ),
    )(
        *(
            pltpu.with_memory_space_constraint(x, pltpu.HBM)
            for x in (
                matrix_state,
                matrix_perm,
                frac_state.reshape(2, seg_rows, LANES),
                frac_aperture.reshape(seg_rows, LANES),
                link_cell[0, 0],
                link_seg[0, 0],
                link_trans[0, 0],
                link_count[0],
                link_upwind[:, 0, 0],
            )
        )
    )
    matrix_out, frac_out = pl.pallas_call(
        write_out,
        out_shape=(
            jax.ShapeDtypeStruct(matrix_state.shape, F32),
            jax.ShapeDtypeStruct((2, seg_rows, LANES), F32),
        ),
        in_specs=[vmem] * 2,
        out_specs=(hbm, hbm),
        scratch_shapes=[dma((2,))],
        compiler_params=pltpu.CompilerParams(vmem_limit_bytes=4 * 1024 * 1024),
    )(matrix_out, frac_out)
    return matrix_out, frac_out.reshape(2, 1, segs)


def solution(mesh):
    return jax.shard_map(
        on_device,
        mesh=mesh,
        in_specs=(
            P(None, "grp", "frac"),
            P("grp", "frac"),
            P(None, "grp", "frac"),
            P("grp", "frac"),
            P("grp", "frac", None, None),
            P("grp", "frac", None, None),
            P("grp", "frac", None, None),
            P("grp", "frac", None),
            P(None, "grp", "frac", None, None),
        ),
        out_specs=(P(None, "grp", "frac"), P(None, "grp", "frac")),
        check_vma=False,
    )
```

```python
import functools

import jax
import jax.numpy as jnp
from jax import lax
from jax.experimental import pallas as pl
from jax.experimental.pallas import tpu as pltpu
from jax.sharding import PartitionSpec as P

ITERS = 3
SWEEPS = 4
LOW_BOUND = 0.02
HIGH_BOUND = 1.98
TAU_STEP = 0.5
MOBILITY_FLOOR = 0.2

F32 = jnp.float32
BF16 = jnp.bfloat16
MESH = pl.DeviceIdType.MESH
LANES = 128
WIDE = 2048
PER = 4
ROWS = 8
AROUND = ((-1, 0), (1, 0), (0, -1), (0, 1), (-1, -1), (-1, 1), (1, -1), (1, 1))


def pieces(value):
    high = value.astype(BF16)
    low = (value - high.astype(F32)).astype(BF16)
    return high, low


def one_hot(index, count):
    ids = lax.broadcasted_iota(jnp.int32, (count, index.shape[1]), 0)
    return jnp.where(ids == index, F32(1.0), F32(0.0)).astype(BF16)


def spread(hot, values):
    rows, count = hot.shape
    stacked = hot.reshape(rows // 16, 16, count)
    out = []
    for value in values:
        for part in pieces(jnp.broadcast_to(value, (16, count))):
            out.append((stacked * part[None]).reshape(rows, count))
    return jnp.concatenate(out, axis=0)


def flux_terms(trans, upwind, cell_p, cell_s, seg_p, seg_s):
    u = jnp.where(upwind > 0.5, cell_s, seg_s)
    weight = trans * (MOBILITY_FLOOR + u * u)
    return weight, weight * (cell_p - seg_p) * u


def kernel(
    groups,
    members,
    cap,
    state_in,
    perm_in,
    frac_in,
    aperture_in,
    cell_in,
    seg_in,
    trans_in,
    count_in,
    upwind_in,
    matrix_out,
    frac_out,
    perm_ref,
    aperture_ref,
    cell_ref,
    seg_ref,
    trans_ref,
    count_ref,
    upwind_ref,
    seg_send,
    seg_recv,
    p_send,
    p_recv,
    f_send,
    f_recv,
    edges,
    fields,
    sat,
    fq,
    side_send,
    halo_row,
    halo_col,
    col_hot,
    row_hot,
    low_hot,
    high_hot,
    cell_acc,
    lost_acc,
    seg_acc,
    held,
    ext_x,
    ext_inv,
    ext_c,
    seg_ss,
    seg_rs,
    p_ss,
    p_rs,
    f_ss,
    f_rs,
    edge_ss,
    edge_rs,
    halo_ss,
    halo_rs,
    load_sem,
):
    g = lax.axis_index("grp")
    me = lax.axis_index("frac")
    slots = members * cap
    rows, cols = perm_ref.shape
    seg_rows = aperture_ref.shape[0]
    per = min(members, PER)
    lines = members // per
    mine = lax.div(me, per)

    def nearest(j):
        return j + (j // 2) * (1 - 2 * (j % 2)) if lines == 4 else j

    def line(step):
        return lax.rem(mine + step + lines, lines)

    def member(step):
        return lax.rem(me + step + members, members)

    def neighbour(step):
        return (lax.rem(g + step[0] + groups, groups), member(step[1]))

    loads = [
        pltpu.make_async_copy(src, dst, load_sem.at[i])
        for i, (src, dst) in enumerate(
            (
                (seg_in, seg_ref),
                (cell_in, cell_ref),
                (count_in, count_ref),
                (trans_in, trans_ref),
                (upwind_in, upwind_ref),
                (state_in.at[0], fields.at[0, 0]),
                (state_in.at[1], sat),
                (frac_in, fq.at[0]),
                (perm_in, perm_ref),
                (aperture_in, aperture_ref),
            )
        )
    ]
    for load in loads:
        load.start()

    barrier = pltpu.get_barrier_semaphore()
    for k in range(1, members):
        pl.semaphore_signal(barrier, inc=1, device_id=(g, member(k)), device_id_type=MESH)
    apart = [step for step in AROUND if step[0] != 0]
    for step in apart:
        pl.semaphore_signal(barrier, inc=1, device_id=neighbour(step), device_id_type=MESH)

    def lanes(block, width):
        return pl.ds(pl.multiple_of(block * width, width), width)

    loads[0].wait()
    seg_float = seg_ref[...].astype(F32)
    for o in range(members):
        seg_send[0:1, o * cap : (o + 1) * cap] = seg_float[o : o + 1, :]

    pl.semaphore_wait(barrier, members - 1 + len(apart))

    def distance(k):
        return lax.rem(lax.div(member(k), per) - mine + lines, lines)

    def exchange(send, recv, send_sem, recv_sem, k):
        to = member(k)
        return pltpu.make_async_remote_copy(
            src_ref=send.at[:, lanes(to, cap)],
            dst_ref=recv.at[:, lanes(me, cap)],
            send_sem=send_sem,
            recv_sem=recv_sem,
            device_id=(g, to),
            device_id_type=MESH,
        )

    def seg_copy(k):
        return exchange(seg_send, seg_recv, seg_ss, seg_rs.at[distance(k)], k)

    def p_copy(t, k):
        return exchange(p_send.at[t], p_recv.at[t], p_ss.at[t], p_rs.at[t], k)

    def f_copy(t, k):
        return exchange(f_send.at[t], f_recv.at[t], f_ss.at[t], f_rs.at[t, distance(k)], k)

    def total(ref, send_sem, recv_sem):
        return pltpu.make_async_remote_copy(
            src_ref=ref,
            dst_ref=ref,
            send_sem=send_sem,
            recv_sem=recv_sem,
            device_id=(g, member(1)),
            device_id_type=MESH,
        )

    others = slots - cap

    def seg_all():
        return total(seg_recv.at[:, :others], seg_ss, seg_rs.at[0])

    def p_all(t):
        return total(p_recv.at[t, :, :others], p_ss.at[t], p_rs.at[t])

    def f_all(t):
        return total(f_recv.at[t, :, :others], f_ss.at[t], f_rs.at[t, 0])

    def wait_line(j, recv, send_sem, recv_sems):
        @pl.when(j == 0)
        def _():
            total(recv.at[:, : (per - 1) * cap], send_sem, recv_sems.at[0]).wait_recv()

        if lines > 1:

            @pl.when(j > 0)
            def _():
                total(recv.at[:, : per * cap], send_sem, recv_sems.at[nearest(j)]).wait_recv()

    def edge_all(t):
        return total(edges.at[t], edge_ss.at[t], edge_rs.at[t])

    def halo_all(t):
        return (
            total(halo_row.at[t], halo_ss.at[t, 0], halo_rs.at[t, 0]),
            total(halo_col.at[t], halo_ss.at[t, 1], halo_rs.at[t, 1]),
        )

    def each(body):
        lax.fori_loop(1, members, lambda k, c: (body(k), c)[1], 0)

    each(lambda k: seg_copy(k).start())
    seg_recv[:, lanes(me, cap)] = seg_send[:, lanes(me, cap)]

    for load in loads[1:5]:
        load.wait()
    eye = lax.broadcasted_iota(jnp.int32, (members, members), 0) == lax.broadcasted_iota(
        jnp.int32, (members, members), 1
    )
    counts = jnp.sum(
        jnp.where(eye, jnp.broadcast_to(count_ref[...].astype(F32), (members, members)), 0.0),
        axis=1,
        keepdims=True,
    )
    place = lax.broadcasted_iota(jnp.int32, (members, cap), 1).astype(F32)
    live_trans = jnp.where(place < counts, trans_ref[...], F32(0.0))
    for t in range(ITERS):
        up = upwind_ref[t].astype(F32)
        for o in range(members):
            here = slice(o * cap, (o + 1) * cap)
            p_send[t, 2:3, here] = up[o : o + 1, :]
            p_send[t, 3:4, here] = live_trans[o : o + 1, :]

    def edge_copies(t):
        return (
            pltpu.make_async_remote_copy(
                src_ref=fq.at[t, 0, pl.ds(seg_rows - ROWS, ROWS), :],
                dst_ref=edges.at[t, 0],
                send_sem=edge_ss.at[t],
                recv_sem=edge_rs.at[t],
                device_id=(g, member(1)),
                device_id_type=MESH,
            ),
            pltpu.make_async_remote_copy(
                src_ref=fq.at[t, 0, pl.ds(0, ROWS), :],
                dst_ref=edges.at[t, 1],
                send_sem=edge_ss.at[t],
                recv_sem=edge_rs.at[t],
                device_id=(g, member(-1)),
                device_id_type=MESH,
            ),
        )

    def halo_copies(t):
        out = []
        for i, (dr, dc) in enumerate(AROUND):
            kind = 0 if dc == 0 else 1
            if dr == 0:
                src = side_send.at[t, i - 2]
                dst = halo_col.at[t, i - 2]
            else:
                edge = pl.ds(0 if dr < 0 else rows - ROWS, ROWS)
                if dc == 0:
                    src = fields.at[t, :, edge, :]
                    dst = halo_row.at[t, i]
                else:
                    src = fields.at[t, :, edge, pl.ds(0 if dc < 0 else cols - LANES, LANES)]
                    dst = halo_col.at[t, i - 2]
            out.append(
                pltpu.make_async_remote_copy(
                    src_ref=src,
                    dst_ref=dst,
                    send_sem=halo_ss.at[t, kind],
                    recv_sem=halo_rs.at[t, kind],
                    device_id=neighbour((dr, dc)),
                    device_id_type=MESH,
                )
            )
        return out

    for load in loads[5:]:
        load.wait()

    def cell_hots(o, carry):
        index = cell_ref[pl.ds(o, 1), :]
        col_hot[:, lanes(o, cap)] = one_hot(lax.rem(index, cols), cols)
        row_hot[:, lanes(o, cap)] = one_hot(lax.div(index, cols), rows)
        return carry

    lax.fori_loop(0, members, cell_hots, 0)

    def gather(per, table, hot_cols, hot_rows, add, send, recv, copy, t, block=None):
        height = hot_rows.shape[0]

        def body(j, carry):
            if block is not None:
                q = block(j)
            elif per == members:
                q = 0
            else:
                q = line(nearest(lines - 1 - j))
            here = lanes(q, per * cap)
            picked = add(jnp.dot(table, hot_cols(here), preferred_element_type=F32))
            hot = hot_rows[:, here].astype(F32)
            for f in range(2):
                send[t, f : f + 1, here] = jnp.sum(
                    picked[f * height : (f + 1) * height] * hot, axis=0, keepdims=True
                )
            for i in range(per):
                k = lax.rem(q * per + i - me + members, members)

                @pl.when(k > 0)
                def _():
                    copy(t, k).start()

            return carry

        lax.fori_loop(0, members // per, body, 0)
        recv[t, :, lanes(me, cap)] = send[t, :, lanes(me, cap)]

    def gather_segments(t, size, block=None):
        for copy in edge_copies(t):
            copy.start()
        table = jnp.concatenate(
            [jnp.concatenate(pieces(fq[t, f]), axis=1) for f in range(2)], axis=0
        )

        def both(here):
            low = low_hot[:, here]
            return jnp.concatenate([low, low], axis=0)

        gather(size, table, both, high_hot, lambda x: x, f_send, f_recv, f_copy, t, block)

    def next_line(j):
        wait_line(j, seg_recv, seg_ss, seg_rs)
        q = line(-nearest(j))
        here = lanes(q, per * cap)
        index = seg_recv[:, here].astype(jnp.int32)
        low_hot[:, here] = one_hot(lax.rem(index, LANES), LANES)
        high_hot[:, here] = one_hot(lax.div(index, LANES), seg_rows)
        return q

    def gather_cells(t):
        highs, lows = zip(pieces(fields[t, 0]), pieces(sat[...]))
        table = jnp.concatenate(highs + lows, axis=0)
        gather(
            per,
            table,
            lambda here: col_hot[:, here],
            row_hot,
            lambda x: x[: 2 * rows] + x[2 * rows :],
            p_send,
            p_recv,
            p_copy,
            t,
        )

    def collect(width, acc, hot_rows, hot_cols, values_of, block=lambda j: j):
        acc[...] = jnp.zeros_like(acc)

        def body(j, carry):
            here = lanes(block(j), width)
            left = spread(hot_rows[:, here], values_of(here))
            acc[...] += lax.dot_general(
                left, hot_cols[:, here], (((1,), (1,)), ((), ())), preferred_element_type=F32
            )
            return carry

        lax.fori_loop(0, slots // width, body, 0)
        height = hot_rows.shape[0]
        return [
            acc[2 * f * height : (2 * f + 1) * height]
            + acc[(2 * f + 1) * height : (2 * f + 2) * height]
            for f in range(acc.shape[0] // (2 * height))
        ]

    def terms(cell_side, seg_side, t, here):
        cell_p = cell_side[t, 0:1, here]
        seg_p = seg_side[t, 0:1, here]
        weight, water = flux_terms(
            cell_side[t, 3:4, here],
            cell_side[t, 2:3, here],
            cell_p,
            cell_side[t, 1:2, here],
            seg_p,
            seg_side[t, 1:2, here],
        )
        return cell_p, seg_p, weight, water

    def scatter_cells(t):
        def values_of(here):
            _, seg_p, weight, _ = terms(p_send, f_recv, t, here)
            return weight, weight * seg_p

        def arrived(j):
            wait_line(j, f_recv.at[t], f_ss.at[t], f_rs.at[t])
            return line(-nearest(j))

        couple, source = collect(per * cap, cell_acc, row_hot, col_hot, values_of, arrived)
        perm = perm_ref[...]
        p = fields[t, 0]
        inverse = 1.0 / (4.0 + perm + couple)
        scaled = inverse * (perm * p + source)
        held[...] = perm + couple
        fields[t, 1] = inverse
        fields[t, 2] = scaled
        copies = halo_copies(t)
        for copy in copies[:2] + copies[4:]:
            copy.start()
        for f, field in enumerate((p, inverse, scaled)):
            side_send[t, 0, f] = jnp.transpose(field[:, :LANES])[:ROWS]
            side_send[t, 1, f] = jnp.transpose(field[:, cols - LANES :])[LANES - ROWS :]
        for copy in copies[2:4]:
            copy.start()

    def scatter_lost(t):
        def values_of(here):
            return (terms(p_send, f_recv, t, here)[3],)

        (lost,) = collect(min(slots, WIDE), lost_acc, row_hot, col_hot, values_of)
        sat[...] = sat[...] - TAU_STEP * lost / held[...]

    def scatter_segments(t):
        def values_of(here):
            cell_p, _, weight, water = terms(p_recv, f_send, t, here)
            return weight * cell_p, weight, water

        inflow, conduct, gained = collect(slots, seg_acc, high_hot, low_hot, values_of)
        edge_all(t).wait_recv()
        aperture = aperture_ref[...]
        p = fq[t, 0]
        first = jnp.where(me > 0, edges[t, 0, ROWS - 1 : ROWS, LANES - 1 : LANES], F32(0.0))
        last = jnp.where(me < members - 1, edges[t, 1, 0:1, 0:1], F32(0.0))
        lane = lax.broadcasted_iota(jnp.int32, (seg_rows, LANES), 1)
        row = lax.broadcasted_iota(jnp.int32, (seg_rows, LANES), 0)
        turned = pltpu.roll(p, 1, axis=1)
        left = jnp.where(lane == 0, pltpu.roll(turned, 1, axis=0), turned)
        left = jnp.where((lane == 0) & (row == 0), first, left)
        turned = pltpu.roll(p, LANES - 1, axis=1)
        right = jnp.where(lane == LANES - 1, pltpu.roll(turned, seg_rows - 1, axis=0), turned)
        right = jnp.where((lane == LANES - 1) & (row == seg_rows - 1), last, right)
        fq[t + 1, 0] = (aperture * p + inflow + left + right) / (aperture + conduct + 2.0)
        fq[t + 1, 1] = fq[t, 1] + TAU_STEP * gained / (aperture + conduct)

    def sweeps(t):
        for copy in halo_all(t):
            copy.wait_recv()
        inside = {
            -1: jnp.where(g > 0, F32(1.0), F32(0.0)),
            1: jnp.where(g < groups - 1, F32(1.0), F32(0.0)),
            0: F32(1.0),
        }
        beside = {
            -1: jnp.where(me > 0, F32(1.0), F32(0.0)),
            1: jnp.where(me < members - 1, F32(1.0), F32(0.0)),
        }
        corner = {
            (-dr, -dc): i - 2 for i, (dr, dc) in enumerate(AROUND) if dc != 0
        }
        east = lax.broadcasted_iota(jnp.int32, (ROWS, LANES), 1) < LANES // 2
        filler = jnp.zeros((LANES - 2 * ROWS, LANES), F32)
        for f, ext in enumerate((ext_x, ext_inv, ext_c)):
            ext[0:ROWS, 0:cols] = halo_row[t, 1, f] * inside[-1]
            ext[ROWS : ROWS + rows, 0:cols] = fields[t, f]
            ext[ROWS + rows :, 0:cols] = halo_row[t, 0, f] * inside[1]
            for dr, at in ((-1, slice(0, ROWS)), (1, slice(ROWS + rows, rows + 2 * ROWS))):
                ext[at, cols:] = jnp.where(
                    east,
                    halo_col[t, corner[dr, 1], f] * (inside[dr] * beside[1]),
                    halo_col[t, corner[dr, -1], f] * (inside[dr] * beside[-1]),
                )
            ext[ROWS : ROWS + rows, cols:] = jnp.transpose(
                jnp.concatenate(
                    [
                        halo_col[t, corner[0, 1], f] * beside[1],
                        filler,
                        halo_col[t, corner[0, -1], f] * beside[-1],
                    ],
                    axis=0,
                )
            )

        height, width = ext_x.shape
        inverse = ext_inv[...]
        scaled = ext_c[...]

        def residual_of(x):
            around = (
                pltpu.roll(x, 1, axis=0)
                + pltpu.roll(x, height - 1, axis=0)
                + pltpu.roll(x, 1, axis=1)
                + pltpu.roll(x, width - 1, axis=1)
            )
            return inverse * around + (scaled - x)

        centre = 0.5 * (HIGH_BOUND + LOW_BOUND)
        half_width = 0.5 * (HIGH_BOUND - LOW_BOUND)
        scale_ratio = centre / half_width
        ratio_now = 1.0 / scale_ratio
        x = ext_x[...]
        update = residual_of(x) / centre
        for sweep_index in range(SWEEPS):
            x = x + update
            if sweep_index + 1 < SWEEPS:
                ratio_next = 1.0 / (2.0 * scale_ratio - ratio_now)
                update = ratio_next * ratio_now * update + (
                    2.0 * ratio_next / half_width
                ) * residual_of(x)
                ratio_now = ratio_next
        fields[t + 1, 0] = x[ROWS : ROWS + rows, :cols]

    gather_cells(0)
    gather_segments(0, per, next_line)

    def outer(t, carry):
        scatter_cells(t)
        p_all(t).wait_recv()
        scatter_segments(t)

        @pl.when(t + 1 < ITERS)
        def _():
            gather_segments(t + 1, members)

        scatter_lost(t)
        sweeps(t)

        @pl.when(t + 1 < ITERS)
        def _():
            gather_cells(t + 1)

        return carry

    lax.fori_loop(0, ITERS, outer, 0)

    matrix_out[0] = fields[ITERS, 0]
    matrix_out[1] = sat[...]
    frac_out[...] = fq[ITERS]

    seg_all().wait_send()

    def drain(t, carry):
        for copy in (p_all(t), f_all(t), edge_all(t), *halo_all(t)):
            copy.wait_send()
        return carry

    lax.fori_loop(0, ITERS, drain, 0)


def write_out(matrix_in, frac_in, matrix_out, frac_out, sems):
    copies = (
        pltpu.make_async_copy(matrix_in, matrix_out, sems.at[0]),
        pltpu.make_async_copy(frac_in, frac_out, sems.at[1]),
    )
    for copy in copies:
        copy.start()
    for copy in copies:
        copy.wait()


def on_device(
    matrix_state,
    matrix_perm,
    frac_state,
    frac_aperture,
    link_cell,
    link_seg,
    link_trans,
    link_count,
    link_upwind,
):
    groups = lax.axis_size("grp")
    members, cap = link_cell.shape[2:]
    rows, cols = matrix_perm.shape
    segs = frac_aperture.shape[1]
    seg_rows = segs // LANES
    slots = members * cap
    lines = max(1, members // PER)
    vmem = pl.BlockSpec(memory_space=pltpu.VMEM)
    hbm = pl.BlockSpec(memory_space=pltpu.HBM)
    dma = pltpu.SemaphoreType.DMA
    around = len(AROUND)
    matrix_out, frac_out = pl.pallas_call(
        functools.partial(kernel, groups, members, cap),
        out_shape=(
            jax.ShapeDtypeStruct(matrix_state.shape, F32),
            jax.ShapeDtypeStruct((2, seg_rows, LANES), F32),
        ),
        in_specs=[hbm] * 9,
        out_specs=(vmem, vmem),
        scratch_shapes=[
            pltpu.VMEM((rows, cols), F32),
            pltpu.VMEM((seg_rows, LANES), F32),
            pltpu.VMEM((members, cap), jnp.int32),
            pltpu.VMEM((members, cap), jnp.int32),
            pltpu.VMEM((members, cap), F32),
            pltpu.VMEM((1, members), jnp.int32),
            pltpu.VMEM((ITERS, members, cap), jnp.int32),
            pltpu.VMEM((1, slots), F32),
            pltpu.VMEM((1, slots), F32),
            pltpu.VMEM((ITERS, 4, slots), F32),
            pltpu.VMEM((ITERS, 4, slots), F32),
            pltpu.VMEM((ITERS, 2, slots), F32),
            pltpu.VMEM((ITERS, 2, slots), F32),
            pltpu.VMEM((ITERS, 2, ROWS, LANES), F32),
            pltpu.VMEM((ITERS + 1, 3, rows, cols), F32),
            pltpu.VMEM((rows, cols), F32),
            pltpu.VMEM((ITERS + 1, 2, seg_rows, LANES), F32),
            pltpu.VMEM((ITERS, 2, 3, ROWS, LANES), F32),
            pltpu.VMEM((ITERS, 2, 3, ROWS, cols), F32),
            pltpu.VMEM((ITERS, 6, 3, ROWS, LANES), F32),
            pltpu.VMEM((cols, slots), BF16),
            pltpu.VMEM((rows, slots), BF16),
            pltpu.VMEM((LANES, slots), BF16),
            pltpu.VMEM((seg_rows, slots), BF16),
            pltpu.VMEM((4 * rows, cols), F32),
            pltpu.VMEM((2 * rows, cols), F32),
            pltpu.VMEM((6 * seg_rows, LANES), F32),
            pltpu.VMEM((rows, cols), F32),
            pltpu.VMEM((rows + 2 * ROWS, cols + LANES), F32),
            pltpu.VMEM((rows + 2 * ROWS, cols + LANES), F32),
            pltpu.VMEM((rows + 2 * ROWS, cols + LANES), F32),
            dma(()),
            dma((lines,)),
            dma((ITERS,)),
            dma((ITERS,)),
            dma((ITERS,)),
            dma((ITERS, lines)),
            dma((ITERS,)),
            dma((ITERS,)),
            dma((ITERS, 2)),
            dma((ITERS, 2)),
            dma((10,)),
        ],
        compiler_params=pltpu.CompilerParams(
            collective_id=0, has_side_effects=True, vmem_limit_bytes=40 * 1024 * 1024
        ),
    )(
        *(
            pltpu.with_memory_space_constraint(x, pltpu.HBM)
            for x in (
                matrix_state,
                matrix_perm,
                frac_state.reshape(2, seg_rows, LANES),
                frac_aperture.reshape(seg_rows, LANES),
                link_cell[0, 0],
                link_seg[0, 0],
                link_trans[0, 0],
                link_count[0],
                link_upwind[:, 0, 0],
            )
        )
    )
    matrix_out, frac_out = pl.pallas_call(
        write_out,
        out_shape=(
            jax.ShapeDtypeStruct(matrix_state.shape, F32),
            jax.ShapeDtypeStruct((2, seg_rows, LANES), F32),
        ),
        in_specs=[vmem] * 2,
        out_specs=(hbm, hbm),
        scratch_shapes=[dma((2,))],
        compiler_params=pltpu.CompilerParams(vmem_limit_bytes=4 * 1024 * 1024),
    )(matrix_out, frac_out)
    return matrix_out, frac_out.reshape(2, 1, segs)


def solution(mesh):
    return jax.shard_map(
        on_device,
        mesh=mesh,
        in_specs=(
            P(None, "grp", "frac"),
            P("grp", "frac"),
            P(None, "grp", "frac"),
            P("grp", "frac"),
            P("grp", "frac", None, None),
            P("grp", "frac", None, None),
            P("grp", "frac", None, None),
            P("grp", "frac", None),
            P(None, "grp", "frac", None, None),
        ),
        out_specs=(P(None, "grp", "frac"), P(None, "grp", "frac")),
        check_vma=False,
    )
```

```python
import functools

import jax
import jax.numpy as jnp
from jax import lax
from jax.experimental import pallas as pl
from jax.experimental.pallas import tpu as pltpu
from jax.sharding import PartitionSpec as P

ITERS = 3
SWEEPS = 4
LOW_BOUND = 0.02
HIGH_BOUND = 1.98
TAU_STEP = 0.5
MOBILITY_FLOOR = 0.2

F32 = jnp.float32
BF16 = jnp.bfloat16
MESH = pl.DeviceIdType.MESH
LANES = 128
WIDE = 2048
PER = 4
ROWS = 8
AROUND = ((-1, 0), (1, 0), (0, -1), (0, 1), (-1, -1), (-1, 1), (1, -1), (1, 1))


def pieces(value):
    high = value.astype(BF16)
    low = (value - high.astype(F32)).astype(BF16)
    return high, low


def one_hot(index, count):
    ids = lax.broadcasted_iota(jnp.int32, (count, index.shape[1]), 0)
    return jnp.where(ids == index, F32(1.0), F32(0.0)).astype(BF16)


def spread(hot, values):
    rows, count = hot.shape
    stacked = hot.reshape(rows // 16, 16, count)
    out = []
    for value in values:
        for part in pieces(jnp.broadcast_to(value, (16, count))):
            out.append((stacked * part[None]).reshape(rows, count))
    return jnp.concatenate(out, axis=0)


def flux_terms(trans, upwind, cell_p, cell_s, seg_p, seg_s):
    u = jnp.where(upwind > 0.5, cell_s, seg_s)
    weight = trans * (MOBILITY_FLOOR + u * u)
    return weight, weight * (cell_p - seg_p) * u


def kernel(
    groups,
    members,
    cap,
    state_in,
    perm_in,
    frac_in,
    aperture_in,
    cell_in,
    seg_in,
    trans_in,
    count_in,
    upwind_in,
    matrix_out,
    frac_out,
    perm_ref,
    aperture_ref,
    cell_ref,
    seg_ref,
    trans_ref,
    count_ref,
    upwind_ref,
    seg_send,
    seg_recv,
    p_send,
    p_recv,
    f_send,
    f_recv,
    edges,
    fields,
    sat,
    fq,
    side_send,
    halo_row,
    halo_col,
    col_hot,
    row_hot,
    low_hot,
    high_hot,
    cell_acc,
    lost_acc,
    seg_acc,
    held,
    ext_x,
    ext_inv,
    ext_c,
    seg_ss,
    seg_rs,
    p_ss,
    p_rs,
    f_ss,
    f_rs,
    edge_ss,
    edge_rs,
    halo_ss,
    halo_rs,
    load_sem,
):
    g = lax.axis_index("grp")
    me = lax.axis_index("frac")
    slots = members * cap
    rows, cols = perm_ref.shape
    seg_rows = aperture_ref.shape[0]
    per = min(members, PER)
    lines = members // per
    mine = lax.div(me, per)

    def nearest(j):
        return j + (j // 2) * (1 - 2 * (j % 2)) if lines == 4 else j

    def line(step):
        return lax.rem(mine + step + lines, lines)

    def member(step):
        return lax.rem(me + step + members, members)

    def neighbour(step):
        return (lax.rem(g + step[0] + groups, groups), member(step[1]))

    loads = [
        pltpu.make_async_copy(src, dst, load_sem.at[i])
        for i, (src, dst) in enumerate(
            (
                (seg_in, seg_ref),
                (cell_in, cell_ref),
                (count_in, count_ref),
                (trans_in, trans_ref),
                (upwind_in, upwind_ref),
                (state_in.at[0], fields.at[0, 0]),
                (state_in.at[1], sat),
                (frac_in, fq.at[0]),
                (perm_in, perm_ref),
                (aperture_in, aperture_ref),
            )
        )
    ]
    for load in loads:
        load.start()

    barrier = pltpu.get_barrier_semaphore()
    for k in range(1, members):
        pl.semaphore_signal(barrier, inc=1, device_id=(g, member(k)), device_id_type=MESH)
    apart = [step for step in AROUND if step[0] != 0]
    for step in apart:
        pl.semaphore_signal(barrier, inc=1, device_id=neighbour(step), device_id_type=MESH)

    def lanes(block, width):
        return pl.ds(pl.multiple_of(block * width, width), width)

    loads[0].wait()
    seg_float = seg_ref[...].astype(F32)
    for o in range(members):
        seg_send[0:1, o * cap : (o + 1) * cap] = seg_float[o : o + 1, :]

    pl.semaphore_wait(barrier, members - 1 + len(apart))

    def distance(k):
        return lax.rem(lax.div(member(k), per) - mine + lines, lines)

    def exchange(send, recv, send_sem, recv_sem, k):
        to = member(k)
        return pltpu.make_async_remote_copy(
            src_ref=send.at[:, lanes(to, cap)],
            dst_ref=recv.at[:, lanes(me, cap)],
            send_sem=send_sem,
            recv_sem=recv_sem,
            device_id=(g, to),
            device_id_type=MESH,
        )

    def seg_copy(k):
        return exchange(seg_send, seg_recv, seg_ss, seg_rs.at[distance(k)], k)

    def p_copy(t, k):
        return exchange(p_send.at[t], p_recv.at[t], p_ss.at[t], p_rs.at[t], k)

    def f_copy(t, k):
        return exchange(f_send.at[t], f_recv.at[t], f_ss.at[t], f_rs.at[t, distance(k)], k)

    def total(ref, send_sem, recv_sem):
        return pltpu.make_async_remote_copy(
            src_ref=ref,
            dst_ref=ref,
            send_sem=send_sem,
            recv_sem=recv_sem,
            device_id=(g, member(1)),
            device_id_type=MESH,
        )

    others = slots - cap

    def seg_all():
        return total(seg_recv.at[:, :others], seg_ss, seg_rs.at[0])

    def p_all(t):
        return total(p_recv.at[t, :, :others], p_ss.at[t], p_rs.at[t])

    def f_all(t):
        return total(f_recv.at[t, :, :others], f_ss.at[t], f_rs.at[t, 0])

    def wait_line(j, recv, send_sem, recv_sems):
        @pl.when(j == 0)
        def _():
            total(recv.at[:, : (per - 1) * cap], send_sem, recv_sems.at[0]).wait_recv()

        if lines > 1:

            @pl.when(j > 0)
            def _():
                total(recv.at[:, : per * cap], send_sem, recv_sems.at[nearest(j)]).wait_recv()

    def edge_all(t):
        return total(edges.at[t], edge_ss.at[t], edge_rs.at[t])

    def halo_all(t):
        return (
            total(halo_row.at[t], halo_ss.at[t, 0], halo_rs.at[t, 0]),
            total(halo_col.at[t], halo_ss.at[t, 1], halo_rs.at[t, 1]),
        )

    def each(body):
        lax.fori_loop(1, members, lambda k, c: (body(k), c)[1], 0)

    each(lambda k: seg_copy(k).start())
    seg_recv[:, lanes(me, cap)] = seg_send[:, lanes(me, cap)]

    for load in loads[1:5]:
        load.wait()
    eye = lax.broadcasted_iota(jnp.int32, (members, members), 0) == lax.broadcasted_iota(
        jnp.int32, (members, members), 1
    )
    counts = jnp.sum(
        jnp.where(eye, jnp.broadcast_to(count_ref[...].astype(F32), (members, members)), 0.0),
        axis=1,
        keepdims=True,
    )
    place = lax.broadcasted_iota(jnp.int32, (members, cap), 1).astype(F32)
    live_trans = jnp.where(place < counts, trans_ref[...], F32(0.0))
    for t in range(ITERS):
        up = upwind_ref[t].astype(F32)
        for o in range(members):
            here = slice(o * cap, (o + 1) * cap)
            p_send[t, 2:3, here] = up[o : o + 1, :]
            p_send[t, 3:4, here] = live_trans[o : o + 1, :]

    def edge_copies(t):
        return (
            pltpu.make_async_remote_copy(
                src_ref=fq.at[t, 0, pl.ds(seg_rows - ROWS, ROWS), :],
                dst_ref=edges.at[t, 0],
                send_sem=edge_ss.at[t],
                recv_sem=edge_rs.at[t],
                device_id=(g, member(1)),
                device_id_type=MESH,
            ),
            pltpu.make_async_remote_copy(
                src_ref=fq.at[t, 0, pl.ds(0, ROWS), :],
                dst_ref=edges.at[t, 1],
                send_sem=edge_ss.at[t],
                recv_sem=edge_rs.at[t],
                device_id=(g, member(-1)),
                device_id_type=MESH,
            ),
        )

    def halo_copies(t):
        out = []
        for i, (dr, dc) in enumerate(AROUND):
            kind = 0 if dc == 0 else 1
            if dr == 0:
                src = side_send.at[t, i - 2]
                dst = halo_col.at[t, i - 2]
            else:
                edge = pl.ds(0 if dr < 0 else rows - ROWS, ROWS)
                if dc == 0:
                    src = fields.at[t, :, edge, :]
                    dst = halo_row.at[t, i]
                else:
                    src = fields.at[t, :, edge, pl.ds(0 if dc < 0 else cols - LANES, LANES)]
                    dst = halo_col.at[t, i - 2]
            out.append(
                pltpu.make_async_remote_copy(
                    src_ref=src,
                    dst_ref=dst,
                    send_sem=halo_ss.at[t, kind],
                    recv_sem=halo_rs.at[t, kind],
                    device_id=neighbour((dr, dc)),
                    device_id_type=MESH,
                )
            )
        return out

    for load in loads[5:]:
        load.wait()

    def cell_hots(o, carry):
        index = cell_ref[pl.ds(o, 1), :]
        col_hot[:, lanes(o, cap)] = one_hot(lax.rem(index, cols), cols)
        row_hot[:, lanes(o, cap)] = one_hot(lax.div(index, cols), rows)
        return carry

    lax.fori_loop(0, members, cell_hots, 0)

    def gather(per, table, hot_cols, hot_rows, add, send, recv, copy, t, block=None):
        height = hot_rows.shape[0]

        def body(j, carry):
            if block is not None:
                q = block(j)
            elif per == members:
                q = 0
            else:
                q = line(nearest(lines - 1 - j))
            here = lanes(q, per * cap)
            picked = add(jnp.dot(table, hot_cols(here), preferred_element_type=F32))
            hot = hot_rows[:, here].astype(F32)
            for f in range(2):
                send[t, f : f + 1, here] = jnp.sum(
                    picked[f * height : (f + 1) * height] * hot, axis=0, keepdims=True
                )
            for i in range(per):
                k = lax.rem(q * per + i - me + members, members)

                @pl.when(k > 0)
                def _():
                    copy(t, k).start()

            return carry

        lax.fori_loop(0, members // per, body, 0, unroll=True)
        recv[t, :, lanes(me, cap)] = send[t, :, lanes(me, cap)]

    def gather_segments(t, size, block=None):
        for copy in edge_copies(t):
            copy.start()
        table = jnp.concatenate(
            [jnp.concatenate(pieces(fq[t, f]), axis=1) for f in range(2)], axis=0
        )

        def both(here):
            low = low_hot[:, here]
            return jnp.concatenate([low, low], axis=0)

        gather(size, table, both, high_hot, lambda x: x, f_send, f_recv, f_copy, t, block)

    def next_line(j):
        wait_line(j, seg_recv, seg_ss, seg_rs)
        q = line(-nearest(j))
        here = lanes(q, per * cap)
        index = seg_recv[:, here].astype(jnp.int32)
        low_hot[:, here] = one_hot(lax.rem(index, LANES), LANES)
        high_hot[:, here] = one_hot(lax.div(index, LANES), seg_rows)
        return q

    def gather_cells(t):
        highs, lows = zip(pieces(fields[t, 0]), pieces(sat[...]))
        table = jnp.concatenate(highs + lows, axis=0)
        gather(
            per,
            table,
            lambda here: col_hot[:, here],
            row_hot,
            lambda x: x[: 2 * rows] + x[2 * rows :],
            p_send,
            p_recv,
            p_copy,
            t,
        )

    def collect(width, acc, hot_rows, hot_cols, values_of, block=lambda j: j):
        acc[...] = jnp.zeros_like(acc)

        def body(j, carry):
            here = lanes(block(j), width)
            left = spread(hot_rows[:, here], values_of(here))
            acc[...] += lax.dot_general(
                left, hot_cols[:, here], (((1,), (1,)), ((), ())), preferred_element_type=F32
            )
            return carry

        lax.fori_loop(0, slots // width, body, 0)
        height = hot_rows.shape[0]
        return [
            acc[2 * f * height : (2 * f + 1) * height]
            + acc[(2 * f + 1) * height : (2 * f + 2) * height]
            for f in range(acc.shape[0] // (2 * height))
        ]

    def terms(cell_side, seg_side, t, here):
        cell_p = cell_side[t, 0:1, here]
        seg_p = seg_side[t, 0:1, here]
        weight, water = flux_terms(
            cell_side[t, 3:4, here],
            cell_side[t, 2:3, here],
            cell_p,
            cell_side[t, 1:2, here],
            seg_p,
            seg_side[t, 1:2, here],
        )
        return cell_p, seg_p, weight, water

    def scatter_cells(t):
        def values_of(here):
            _, seg_p, weight, _ = terms(p_send, f_recv, t, here)
            return weight, weight * seg_p

        def arrived(j):
            wait_line(j, f_recv.at[t], f_ss.at[t], f_rs.at[t])
            return line(-nearest(j))

        couple, source = collect(per * cap, cell_acc, row_hot, col_hot, values_of, arrived)
        perm = perm_ref[...]
        p = fields[t, 0]
        inverse = 1.0 / (4.0 + perm + couple)
        scaled = inverse * (perm * p + source)
        held[...] = perm + couple
        fields[t, 1] = inverse
        fields[t, 2] = scaled
        copies = halo_copies(t)
        for copy in copies[:2] + copies[4:]:
            copy.start()
        for f, field in enumerate((p, inverse, scaled)):
            side_send[t, 0, f] = jnp.transpose(field[:, :LANES])[:ROWS]
            side_send[t, 1, f] = jnp.transpose(field[:, cols - LANES :])[LANES - ROWS :]
        for copy in copies[2:4]:
            copy.start()

    def scatter_lost(t):
        def values_of(here):
            return (terms(p_send, f_recv, t, here)[3],)

        (lost,) = collect(min(slots, WIDE), lost_acc, row_hot, col_hot, values_of)
        sat[...] = sat[...] - TAU_STEP * lost / held[...]

    def scatter_segments(t):
        def values_of(here):
            cell_p, _, weight, water = terms(p_recv, f_send, t, here)
            return weight * cell_p, weight, water

        inflow, conduct, gained = collect(slots, seg_acc, high_hot, low_hot, values_of)
        edge_all(t).wait_recv()
        aperture = aperture_ref[...]
        p = fq[t, 0]
        first = jnp.where(me > 0, edges[t, 0, ROWS - 1 : ROWS, LANES - 1 : LANES], F32(0.0))
        last = jnp.where(me < members - 1, edges[t, 1, 0:1, 0:1], F32(0.0))
        lane = lax.broadcasted_iota(jnp.int32, (seg_rows, LANES), 1)
        row = lax.broadcasted_iota(jnp.int32, (seg_rows, LANES), 0)
        turned = pltpu.roll(p, 1, axis=1)
        left = jnp.where(lane == 0, pltpu.roll(turned, 1, axis=0), turned)
        left = jnp.where((lane == 0) & (row == 0), first, left)
        turned = pltpu.roll(p, LANES - 1, axis=1)
        right = jnp.where(lane == LANES - 1, pltpu.roll(turned, seg_rows - 1, axis=0), turned)
        right = jnp.where((lane == LANES - 1) & (row == seg_rows - 1), last, right)
        fq[t + 1, 0] = (aperture * p + inflow + left + right) / (aperture + conduct + 2.0)
        fq[t + 1, 1] = fq[t, 1] + TAU_STEP * gained / (aperture + conduct)

    def sweeps(t):
        for f, ext in enumerate((ext_x, ext_inv, ext_c)):
            ext[ROWS : ROWS + rows, 0:cols] = fields[t, f]
        for copy in halo_all(t):
            copy.wait_recv()
        inside = {
            -1: jnp.where(g > 0, F32(1.0), F32(0.0)),
            1: jnp.where(g < groups - 1, F32(1.0), F32(0.0)),
            0: F32(1.0),
        }
        beside = {
            -1: jnp.where(me > 0, F32(1.0), F32(0.0)),
            1: jnp.where(me < members - 1, F32(1.0), F32(0.0)),
        }
        corner = {
            (-dr, -dc): i - 2 for i, (dr, dc) in enumerate(AROUND) if dc != 0
        }
        east = lax.broadcasted_iota(jnp.int32, (ROWS, LANES), 1) < LANES // 2
        filler = jnp.zeros((LANES - 2 * ROWS, LANES), F32)
        for f, ext in enumerate((ext_x, ext_inv, ext_c)):
            ext[0:ROWS, 0:cols] = halo_row[t, 1, f] * inside[-1]
            ext[ROWS + rows :, 0:cols] = halo_row[t, 0, f] * inside[1]
            for dr, at in ((-1, slice(0, ROWS)), (1, slice(ROWS + rows, rows + 2 * ROWS))):
                ext[at, cols:] = jnp.where(
                    east,
                    halo_col[t, corner[dr, 1], f] * (inside[dr] * beside[1]),
                    halo_col[t, corner[dr, -1], f] * (inside[dr] * beside[-1]),
                )
            ext[ROWS : ROWS + rows, cols:] = jnp.transpose(
                jnp.concatenate(
                    [
                        halo_col[t, corner[0, 1], f] * beside[1],
                        filler,
                        halo_col[t, corner[0, -1], f] * beside[-1],
                    ],
                    axis=0,
                )
            )

        height, width = ext_x.shape
        inverse = ext_inv[...]
        scaled = ext_c[...]

        def residual_of(x):
            around = (
                pltpu.roll(x, 1, axis=0)
                + pltpu.roll(x, height - 1, axis=0)
                + pltpu.roll(x, 1, axis=1)
                + pltpu.roll(x, width - 1, axis=1)
            )
            return inverse * around + (scaled - x)

        centre = 0.5 * (HIGH_BOUND + LOW_BOUND)
        half_width = 0.5 * (HIGH_BOUND - LOW_BOUND)
        scale_ratio = centre / half_width
        ratio_now = 1.0 / scale_ratio
        x = ext_x[...]
        update = residual_of(x) / centre
        for sweep_index in range(SWEEPS):
            x = x + update
            if sweep_index + 1 < SWEEPS:
                ratio_next = 1.0 / (2.0 * scale_ratio - ratio_now)
                update = ratio_next * ratio_now * update + (
                    2.0 * ratio_next / half_width
                ) * residual_of(x)
                ratio_now = ratio_next
        fields[t + 1, 0] = x[ROWS : ROWS + rows, :cols]

    gather_cells(0)
    gather_segments(0, per, next_line)

    def outer(t, carry):
        scatter_cells(t)
        p_all(t).wait_recv()
        scatter_segments(t)

        @pl.when(t + 1 < ITERS)
        def _():
            gather_segments(t + 1, members)

        scatter_lost(t)
        sweeps(t)

        @pl.when(t + 1 < ITERS)
        def _():
            gather_cells(t + 1)

        return carry

    for t in range(ITERS):
        outer(t, 0)

    matrix_out[0] = fields[ITERS, 0]
    matrix_out[1] = sat[...]
    frac_out[...] = fq[ITERS]

    seg_all().wait_send()

    def drain(t, carry):
        for copy in (p_all(t), f_all(t), edge_all(t), *halo_all(t)):
            copy.wait_send()
        return carry

    lax.fori_loop(0, ITERS, drain, 0)


def write_out(matrix_in, frac_in, matrix_out, frac_out, sems):
    copies = (
        pltpu.make_async_copy(matrix_in, matrix_out, sems.at[0]),
        pltpu.make_async_copy(frac_in, frac_out, sems.at[1]),
    )
    for copy in copies:
        copy.start()
    for copy in copies:
        copy.wait()


def on_device(
    matrix_state,
    matrix_perm,
    frac_state,
    frac_aperture,
    link_cell,
    link_seg,
    link_trans,
    link_count,
    link_upwind,
):
    groups = lax.axis_size("grp")
    members, cap = link_cell.shape[2:]
    rows, cols = matrix_perm.shape
    segs = frac_aperture.shape[1]
    seg_rows = segs // LANES
    slots = members * cap
    lines = max(1, members // PER)
    vmem = pl.BlockSpec(memory_space=pltpu.VMEM)
    hbm = pl.BlockSpec(memory_space=pltpu.HBM)
    dma = pltpu.SemaphoreType.DMA
    around = len(AROUND)
    matrix_out, frac_out = pl.pallas_call(
        functools.partial(kernel, groups, members, cap),
        out_shape=(
            jax.ShapeDtypeStruct(matrix_state.shape, F32),
            jax.ShapeDtypeStruct((2, seg_rows, LANES), F32),
        ),
        in_specs=[hbm] * 9,
        out_specs=(vmem, vmem),
        scratch_shapes=[
            pltpu.VMEM((rows, cols), F32),
            pltpu.VMEM((seg_rows, LANES), F32),
            pltpu.VMEM((members, cap), jnp.int32),
            pltpu.VMEM((members, cap), jnp.int32),
            pltpu.VMEM((members, cap), F32),
            pltpu.VMEM((1, members), jnp.int32),
            pltpu.VMEM((ITERS, members, cap), jnp.int32),
            pltpu.VMEM((1, slots), F32),
            pltpu.VMEM((1, slots), F32),
            pltpu.VMEM((ITERS, 4, slots), F32),
            pltpu.VMEM((ITERS, 4, slots), F32),
            pltpu.VMEM((ITERS, 2, slots), F32),
            pltpu.VMEM((ITERS, 2, slots), F32),
            pltpu.VMEM((ITERS, 2, ROWS, LANES), F32),
            pltpu.VMEM((ITERS + 1, 3, rows, cols), F32),
            pltpu.VMEM((rows, cols), F32),
            pltpu.VMEM((ITERS + 1, 2, seg_rows, LANES), F32),
            pltpu.VMEM((ITERS, 2, 3, ROWS, LANES), F32),
            pltpu.VMEM((ITERS, 2, 3, ROWS, cols), F32),
            pltpu.VMEM((ITERS, 6, 3, ROWS, LANES), F32),
            pltpu.VMEM((cols, slots), BF16),
            pltpu.VMEM((rows, slots), BF16),
            pltpu.VMEM((LANES, slots), BF16),
            pltpu.VMEM((seg_rows, slots), BF16),
            pltpu.VMEM((4 * rows, cols), F32),
            pltpu.VMEM((2 * rows, cols), F32),
            pltpu.VMEM((6 * seg_rows, LANES), F32),
            pltpu.VMEM((rows, cols), F32),
            pltpu.VMEM((rows + 2 * ROWS, cols + LANES), F32),
            pltpu.VMEM((rows + 2 * ROWS, cols + LANES), F32),
            pltpu.VMEM((rows + 2 * ROWS, cols + LANES), F32),
            dma(()),
            dma((lines,)),
            dma((ITERS,)),
            dma((ITERS,)),
            dma((ITERS,)),
            dma((ITERS, lines)),
            dma((ITERS,)),
            dma((ITERS,)),
            dma((ITERS, 2)),
            dma((ITERS, 2)),
            dma((10,)),
        ],
        compiler_params=pltpu.CompilerParams(
            collective_id=0, has_side_effects=True, vmem_limit_bytes=40 * 1024 * 1024
        ),
    )(
        *(
            pltpu.with_memory_space_constraint(x, pltpu.HBM)
            for x in (
                matrix_state,
                matrix_perm,
                frac_state.reshape(2, seg_rows, LANES),
                frac_aperture.reshape(seg_rows, LANES),
                link_cell[0, 0],
                link_seg[0, 0],
                link_trans[0, 0],
                link_count[0],
                link_upwind[:, 0, 0],
            )
        )
    )
    matrix_out, frac_out = pl.pallas_call(
        write_out,
        out_shape=(
            jax.ShapeDtypeStruct(matrix_state.shape, F32),
            jax.ShapeDtypeStruct((2, seg_rows, LANES), F32),
        ),
        in_specs=[vmem] * 2,
        out_specs=(hbm, hbm),
        scratch_shapes=[dma((2,))],
        compiler_params=pltpu.CompilerParams(vmem_limit_bytes=4 * 1024 * 1024),
    )(matrix_out, frac_out)
    return matrix_out, frac_out.reshape(2, 1, segs)


def solution(mesh):
    return jax.shard_map(
        on_device,
        mesh=mesh,
        in_specs=(
            P(None, "grp", "frac"),
            P("grp", "frac"),
            P(None, "grp", "frac"),
            P("grp", "frac"),
            P("grp", "frac", None, None),
            P("grp", "frac", None, None),
            P("grp", "frac", None, None),
            P("grp", "frac", None),
            P(None, "grp", "frac", None, None),
        ),
        out_specs=(P(None, "grp", "frac"), P(None, "grp", "frac")),
        check_vma=False,
    )
```

```python
import functools

import jax
import jax.numpy as jnp
from jax import lax
from jax.experimental import pallas as pl
from jax.experimental.pallas import tpu as pltpu
from jax.sharding import PartitionSpec as P

ITERS = 3
SWEEPS = 4
LOW_BOUND = 0.02
HIGH_BOUND = 1.98
TAU_STEP = 0.5
MOBILITY_FLOOR = 0.2

F32 = jnp.float32
BF16 = jnp.bfloat16
MESH = pl.DeviceIdType.MESH
LANES = 128
WIDE = 1024
PER = 4
ROWS = 8
AROUND = ((-1, 0), (1, 0), (0, -1), (0, 1), (-1, -1), (-1, 1), (1, -1), (1, 1))


def pieces(value):
    high = value.astype(BF16)
    low = (value - high.astype(F32)).astype(BF16)
    return high, low


def one_hot(index, count):
    ids = lax.broadcasted_iota(jnp.int32, (count, index.shape[1]), 0)
    return jnp.where(ids == index, F32(1.0), F32(0.0)).astype(BF16)


def spread(hot, values):
    rows, count = hot.shape
    stacked = hot.reshape(rows // 16, 16, count)
    out = []
    for value in values:
        for part in pieces(jnp.broadcast_to(value, (16, count))):
            out.append((stacked * part[None]).reshape(rows, count))
    return jnp.concatenate(out, axis=0)


def flux_terms(trans, upwind, cell_p, cell_s, seg_p, seg_s):
    u = jnp.where(upwind > 0.5, cell_s, seg_s)
    weight = trans * (MOBILITY_FLOOR + u * u)
    return weight, weight * (cell_p - seg_p) * u


def kernel(
    groups,
    members,
    cap,
    state_in,
    perm_in,
    frac_in,
    aperture_in,
    cell_in,
    seg_in,
    trans_in,
    count_in,
    upwind_in,
    matrix_out,
    frac_out,
    perm_ref,
    aperture_ref,
    cell_ref,
    seg_ref,
    trans_ref,
    count_ref,
    upwind_ref,
    seg_send,
    seg_recv,
    p_send,
    p_recv,
    f_send,
    f_recv,
    edges,
    fields,
    sat,
    fq,
    side_send,
    halo_row,
    halo_col,
    col_hot,
    row_hot,
    low_hot,
    high_hot,
    cell_acc,
    lost_acc,
    seg_acc,
    held,
    ext_x,
    ext_inv,
    ext_c,
    seg_ss,
    seg_rs,
    p_ss,
    p_rs,
    f_ss,
    f_rs,
    edge_ss,
    edge_rs,
    halo_ss,
    halo_rs,
    load_sem,
):
    g = lax.axis_index("grp")
    me = lax.axis_index("frac")
    slots = members * cap
    rows, cols = perm_ref.shape
    seg_rows = aperture_ref.shape[0]
    per = min(members, PER)
    lines = members // per
    mine = lax.div(me, per)

    def nearest(j):
        return j + (j // 2) * (1 - 2 * (j % 2)) if lines == 4 else j

    def line(step):
        return lax.rem(mine + step + lines, lines)

    def member(step):
        return lax.rem(me + step + members, members)

    def neighbour(step):
        return (lax.rem(g + step[0] + groups, groups), member(step[1]))

    loads = [
        pltpu.make_async_copy(src, dst, load_sem.at[i])
        for i, (src, dst) in enumerate(
            (
                (seg_in, seg_ref),
                (cell_in, cell_ref),
                (count_in, count_ref),
                (trans_in, trans_ref),
                (upwind_in, upwind_ref),
                (state_in.at[0], fields.at[0, 0]),
                (state_in.at[1], sat),
                (frac_in, fq.at[0]),
                (perm_in, perm_ref),
                (aperture_in, aperture_ref),
            )
        )
    ]
    for load in loads:
        load.start()

    barrier = pltpu.get_barrier_semaphore()
    for k in range(1, members):
        pl.semaphore_signal(barrier, inc=1, device_id=(g, member(k)), device_id_type=MESH)
    apart = [step for step in AROUND if step[0] != 0]
    for step in apart:
        pl.semaphore_signal(barrier, inc=1, device_id=neighbour(step), device_id_type=MESH)

    def lanes(block, width):
        return pl.ds(pl.multiple_of(block * width, width), width)

    loads[0].wait()
    seg_float = seg_ref[...].astype(F32)
    for o in range(members):
        seg_send[0:1, o * cap : (o + 1) * cap] = seg_float[o : o + 1, :]

    pl.semaphore_wait(barrier, members - 1 + len(apart))

    def distance(k):
        return lax.rem(lax.div(member(k), per) - mine + lines, lines)

    def exchange(send, recv, send_sem, recv_sem, k):
        to = member(k)
        return pltpu.make_async_remote_copy(
            src_ref=send.at[:, lanes(to, cap)],
            dst_ref=recv.at[:, lanes(me, cap)],
            send_sem=send_sem,
            recv_sem=recv_sem,
            device_id=(g, to),
            device_id_type=MESH,
        )

    def seg_copy(k):
        return exchange(seg_send, seg_recv, seg_ss, seg_rs.at[distance(k)], k)

    def p_copy(t, k):
        return exchange(p_send.at[t], p_recv.at[t], p_ss.at[t], p_rs.at[t], k)

    def f_copy(t, k):
        return exchange(f_send.at[t], f_recv.at[t], f_ss.at[t], f_rs.at[t, distance(k)], k)

    def total(ref, send_sem, recv_sem):
        return pltpu.make_async_remote_copy(
            src_ref=ref,
            dst_ref=ref,
            send_sem=send_sem,
            recv_sem=recv_sem,
            device_id=(g, member(1)),
            device_id_type=MESH,
        )

    others = slots - cap

    def seg_all():
        return total(seg_recv.at[:, :others], seg_ss, seg_rs.at[0])

    def p_all(t):
        return total(p_recv.at[t, :, :others], p_ss.at[t], p_rs.at[t])

    def f_all(t):
        return total(f_recv.at[t, :, :others], f_ss.at[t], f_rs.at[t, 0])

    def wait_line(j, recv, send_sem, recv_sems):
        @pl.when(j == 0)
        def _():
            total(recv.at[:, : (per - 1) * cap], send_sem, recv_sems.at[0]).wait_recv()

        if lines > 1:

            @pl.when(j > 0)
            def _():
                total(recv.at[:, : per * cap], send_sem, recv_sems.at[nearest(j)]).wait_recv()

    def edge_all(t):
        return total(edges.at[t], edge_ss.at[t], edge_rs.at[t])

    def halo_all(t):
        return (
            total(halo_row.at[t], halo_ss.at[t, 0], halo_rs.at[t, 0]),
            total(halo_col.at[t], halo_ss.at[t, 1], halo_rs.at[t, 1]),
        )

    def each(body):
        lax.fori_loop(1, members, lambda k, c: (body(k), c)[1], 0)

    each(lambda k: seg_copy(k).start())
    seg_recv[:, lanes(me, cap)] = seg_send[:, lanes(me, cap)]

    for load in loads[1:5]:
        load.wait()
    eye = lax.broadcasted_iota(jnp.int32, (members, members), 0) == lax.broadcasted_iota(
        jnp.int32, (members, members), 1
    )
    counts = jnp.sum(
        jnp.where(eye, jnp.broadcast_to(count_ref[...].astype(F32), (members, members)), 0.0),
        axis=1,
        keepdims=True,
    )
    place = lax.broadcasted_iota(jnp.int32, (members, cap), 1).astype(F32)
    live_trans = jnp.where(place < counts, trans_ref[...], F32(0.0))
    for t in range(ITERS):
        up = upwind_ref[t].astype(F32)
        for o in range(members):
            here = slice(o * cap, (o + 1) * cap)
            p_send[t, 2:3, here] = up[o : o + 1, :]
            p_send[t, 3:4, here] = live_trans[o : o + 1, :]

    def edge_copies(t):
        return (
            pltpu.make_async_remote_copy(
                src_ref=fq.at[t, 0, pl.ds(seg_rows - ROWS, ROWS), :],
                dst_ref=edges.at[t, 0],
                send_sem=edge_ss.at[t],
                recv_sem=edge_rs.at[t],
                device_id=(g, member(1)),
                device_id_type=MESH,
            ),
            pltpu.make_async_remote_copy(
                src_ref=fq.at[t, 0, pl.ds(0, ROWS), :],
                dst_ref=edges.at[t, 1],
                send_sem=edge_ss.at[t],
                recv_sem=edge_rs.at[t],
                device_id=(g, member(-1)),
                device_id_type=MESH,
            ),
        )

    def halo_copies(t):
        out = []
        for i, (dr, dc) in enumerate(AROUND):
            kind = 0 if dc == 0 else 1
            if dr == 0:
                src = side_send.at[t, i - 2]
                dst = halo_col.at[t, i - 2]
            else:
                edge = pl.ds(0 if dr < 0 else rows - ROWS, ROWS)
                if dc == 0:
                    src = fields.at[t, :, edge, :]
                    dst = halo_row.at[t, i]
                else:
                    src = fields.at[t, :, edge, pl.ds(0 if dc < 0 else cols - LANES, LANES)]
                    dst = halo_col.at[t, i - 2]
            out.append(
                pltpu.make_async_remote_copy(
                    src_ref=src,
                    dst_ref=dst,
                    send_sem=halo_ss.at[t, kind],
                    recv_sem=halo_rs.at[t, kind],
                    device_id=neighbour((dr, dc)),
                    device_id_type=MESH,
                )
            )
        return out

    for load in loads[5:]:
        load.wait()

    def cell_hots(o, carry):
        index = cell_ref[pl.ds(o, 1), :]
        col_hot[:, lanes(o, cap)] = one_hot(lax.rem(index, cols), cols)
        row_hot[:, lanes(o, cap)] = one_hot(lax.div(index, cols), rows)
        return carry

    lax.fori_loop(0, members, cell_hots, 0)

    def gather(per, table, hot_cols, hot_rows, add, send, recv, copy, t, block=None):
        height = hot_rows.shape[0]

        def body(j, carry):
            if block is not None:
                q = block(j)
            elif per == members:
                q = 0
            else:
                q = line(nearest(lines - 1 - j))
            here = lanes(q, per * cap)
            picked = add(jnp.dot(table, hot_cols(here), preferred_element_type=F32))
            hot = hot_rows[:, here].astype(F32)
            for f in range(2):
                send[t, f : f + 1, here] = jnp.sum(
                    picked[f * height : (f + 1) * height] * hot, axis=0, keepdims=True
                )
            for i in range(per):
                k = lax.rem(q * per + i - me + members, members)

                @pl.when(k > 0)
                def _():
                    copy(t, k).start()

            return carry

        lax.fori_loop(0, members // per, body, 0, unroll=True)
        recv[t, :, lanes(me, cap)] = send[t, :, lanes(me, cap)]

    def gather_segments(t, size, block=None):
        for copy in edge_copies(t):
            copy.start()
        table = jnp.concatenate(
            [jnp.concatenate(pieces(fq[t, f]), axis=1) for f in range(2)], axis=0
        )

        def both(here):
            low = low_hot[:, here]
            return jnp.concatenate([low, low], axis=0)

        gather(size, table, both, high_hot, lambda x: x, f_send, f_recv, f_copy, t, block)

    def next_line(j):
        wait_line(j, seg_recv, seg_ss, seg_rs)
        q = line(-nearest(j))
        here = lanes(q, per * cap)
        index = seg_recv[:, here].astype(jnp.int32)
        low_hot[:, here] = one_hot(lax.rem(index, LANES), LANES)
        high_hot[:, here] = one_hot(lax.div(index, LANES), seg_rows)
        return q

    def gather_cells(t):
        highs, lows = zip(pieces(fields[t, 0]), pieces(sat[...]))
        table = jnp.concatenate(highs + lows, axis=0)
        gather(
            per,
            table,
            lambda here: col_hot[:, here],
            row_hot,
            lambda x: x[: 2 * rows] + x[2 * rows :],
            p_send,
            p_recv,
            p_copy,
            t,
        )

    def collect(width, acc, hot_rows, hot_cols, values_of, block=lambda j: j):
        acc[...] = jnp.zeros_like(acc)

        def body(j, carry):
            here = lanes(block(j), width)
            left = spread(hot_rows[:, here], values_of(here))
            acc[...] += lax.dot_general(
                left, hot_cols[:, here], (((1,), (1,)), ((), ())), preferred_element_type=F32
            )
            return carry

        lax.fori_loop(0, slots // width, body, 0)
        height = hot_rows.shape[0]
        return [
            acc[2 * f * height : (2 * f + 1) * height]
            + acc[(2 * f + 1) * height : (2 * f + 2) * height]
            for f in range(acc.shape[0] // (2 * height))
        ]

    def terms(cell_side, seg_side, t, here):
        cell_p = cell_side[t, 0:1, here]
        seg_p = seg_side[t, 0:1, here]
        weight, water = flux_terms(
            cell_side[t, 3:4, here],
            cell_side[t, 2:3, here],
            cell_p,
            cell_side[t, 1:2, here],
            seg_p,
            seg_side[t, 1:2, here],
        )
        return cell_p, seg_p, weight, water

    def scatter_cells(t):
        def values_of(here):
            _, seg_p, weight, _ = terms(p_send, f_recv, t, here)
            return weight, weight * seg_p

        def arrived(j):
            wait_line(j, f_recv.at[t], f_ss.at[t], f_rs.at[t])
            return line(-nearest(j))

        couple, source = collect(per * cap, cell_acc, row_hot, col_hot, values_of, arrived)
        perm = perm_ref[...]
        p = fields[t, 0]
        inverse = 1.0 / (4.0 + perm + couple)
        scaled = inverse * (perm * p + source)
        held[...] = perm + couple
        fields[t, 1] = inverse
        fields[t, 2] = scaled
        copies = halo_copies(t)
        for copy in copies[:2] + copies[4:]:
            copy.start()
        for f, field in enumerate((p, inverse, scaled)):
            side_send[t, 0, f] = jnp.transpose(field[:, :LANES])[:ROWS]
            side_send[t, 1, f] = jnp.transpose(field[:, cols - LANES :])[LANES - ROWS :]
        for copy in copies[2:4]:
            copy.start()

    def scatter_lost(t):
        def values_of(here):
            return (terms(p_send, f_recv, t, here)[3],)

        (lost,) = collect(min(slots, WIDE), lost_acc, row_hot, col_hot, values_of)
        sat[...] = sat[...] - TAU_STEP * lost / held[...]

    def scatter_segments(t):
        def values_of(here):
            cell_p, _, weight, water = terms(p_recv, f_send, t, here)
            return weight * cell_p, weight, water

        inflow, conduct, gained = collect(slots, seg_acc, high_hot, low_hot, values_of)
        edge_all(t).wait_recv()
        aperture = aperture_ref[...]
        p = fq[t, 0]
        first = jnp.where(me > 0, edges[t, 0, ROWS - 1 : ROWS, LANES - 1 : LANES], F32(0.0))
        last = jnp.where(me < members - 1, edges[t, 1, 0:1, 0:1], F32(0.0))
        lane = lax.broadcasted_iota(jnp.int32, (seg_rows, LANES), 1)
        row = lax.broadcasted_iota(jnp.int32, (seg_rows, LANES), 0)
        turned = pltpu.roll(p, 1, axis=1)
        left = jnp.where(lane == 0, pltpu.roll(turned, 1, axis=0), turned)
        left = jnp.where((lane == 0) & (row == 0), first, left)
        turned = pltpu.roll(p, LANES - 1, axis=1)
        right = jnp.where(lane == LANES - 1, pltpu.roll(turned, seg_rows - 1, axis=0), turned)
        right = jnp.where((lane == LANES - 1) & (row == seg_rows - 1), last, right)
        fq[t + 1, 0] = (aperture * p + inflow + left + right) / (aperture + conduct + 2.0)
        fq[t + 1, 1] = fq[t, 1] + TAU_STEP * gained / (aperture + conduct)

    def sweeps(t):
        for f, ext in enumerate((ext_x, ext_inv, ext_c)):
            ext[ROWS : ROWS + rows, 0:cols] = fields[t, f]
        for copy in halo_all(t):
            copy.wait_recv()
        inside = {
            -1: jnp.where(g > 0, F32(1.0), F32(0.0)),
            1: jnp.where(g < groups - 1, F32(1.0), F32(0.0)),
            0: F32(1.0),
        }
        beside = {
            -1: jnp.where(me > 0, F32(1.0), F32(0.0)),
            1: jnp.where(me < members - 1, F32(1.0), F32(0.0)),
        }
        corner = {
            (-dr, -dc): i - 2 for i, (dr, dc) in enumerate(AROUND) if dc != 0
        }
        east = lax.broadcasted_iota(jnp.int32, (ROWS, LANES), 1) < LANES // 2
        filler = jnp.zeros((LANES - 2 * ROWS, LANES), F32)
        for f, ext in enumerate((ext_x, ext_inv, ext_c)):
            ext[0:ROWS, 0:cols] = halo_row[t, 1, f] * inside[-1]
            ext[ROWS + rows :, 0:cols] = halo_row[t, 0, f] * inside[1]
            for dr, at in ((-1, slice(0, ROWS)), (1, slice(ROWS + rows, rows + 2 * ROWS))):
                ext[at, cols:] = jnp.where(
                    east,
                    halo_col[t, corner[dr, 1], f] * (inside[dr] * beside[1]),
                    halo_col[t, corner[dr, -1], f] * (inside[dr] * beside[-1]),
                )
            ext[ROWS : ROWS + rows, cols:] = jnp.transpose(
                jnp.concatenate(
                    [
                        halo_col[t, corner[0, 1], f] * beside[1],
                        filler,
                        halo_col[t, corner[0, -1], f] * beside[-1],
                    ],
                    axis=0,
                )
            )

        height, width = ext_x.shape
        inverse = ext_inv[...]
        scaled = ext_c[...]

        def residual_of(x):
            around = (
                pltpu.roll(x, 1, axis=0)
                + pltpu.roll(x, height - 1, axis=0)
                + pltpu.roll(x, 1, axis=1)
                + pltpu.roll(x, width - 1, axis=1)
            )
            return inverse * around + (scaled - x)

        centre = 0.5 * (HIGH_BOUND + LOW_BOUND)
        half_width = 0.5 * (HIGH_BOUND - LOW_BOUND)
        scale_ratio = centre / half_width
        ratio_now = 1.0 / scale_ratio
        x = ext_x[...]
        update = residual_of(x) / centre
        for sweep_index in range(SWEEPS):
            x = x + update
            if sweep_index + 1 < SWEEPS:
                ratio_next = 1.0 / (2.0 * scale_ratio - ratio_now)
                update = ratio_next * ratio_now * update + (
                    2.0 * ratio_next / half_width
                ) * residual_of(x)
                ratio_now = ratio_next
        fields[t + 1, 0] = x[ROWS : ROWS + rows, :cols]

    gather_cells(0)
    gather_segments(0, per, next_line)

    def outer(t, carry):
        scatter_cells(t)
        p_all(t).wait_recv()
        scatter_segments(t)

        @pl.when(t + 1 < ITERS)
        def _():
            gather_segments(t + 1, members)

        scatter_lost(t)
        sweeps(t)

        @pl.when(t + 1 < ITERS)
        def _():
            gather_cells(t + 1)

        return carry

    for t in range(ITERS):
        outer(t, 0)

    matrix_out[0] = fields[ITERS, 0]
    matrix_out[1] = sat[...]
    frac_out[...] = fq[ITERS]

    seg_all().wait_send()

    def drain(t, carry):
        for copy in (p_all(t), f_all(t), edge_all(t), *halo_all(t)):
            copy.wait_send()
        return carry

    lax.fori_loop(0, ITERS, drain, 0)


def write_out(matrix_in, frac_in, matrix_out, frac_out, sems):
    copies = (
        pltpu.make_async_copy(matrix_in, matrix_out, sems.at[0]),
        pltpu.make_async_copy(frac_in, frac_out, sems.at[1]),
    )
    for copy in copies:
        copy.start()
    for copy in copies:
        copy.wait()


def on_device(
    matrix_state,
    matrix_perm,
    frac_state,
    frac_aperture,
    link_cell,
    link_seg,
    link_trans,
    link_count,
    link_upwind,
):
    groups = lax.axis_size("grp")
    members, cap = link_cell.shape[2:]
    rows, cols = matrix_perm.shape
    segs = frac_aperture.shape[1]
    seg_rows = segs // LANES
    slots = members * cap
    lines = max(1, members // PER)
    vmem = pl.BlockSpec(memory_space=pltpu.VMEM)
    hbm = pl.BlockSpec(memory_space=pltpu.HBM)
    dma = pltpu.SemaphoreType.DMA
    around = len(AROUND)
    matrix_out, frac_out = pl.pallas_call(
        functools.partial(kernel, groups, members, cap),
        out_shape=(
            jax.ShapeDtypeStruct(matrix_state.shape, F32),
            jax.ShapeDtypeStruct((2, seg_rows, LANES), F32),
        ),
        in_specs=[hbm] * 9,
        out_specs=(vmem, vmem),
        scratch_shapes=[
            pltpu.VMEM((rows, cols), F32),
            pltpu.VMEM((seg_rows, LANES), F32),
            pltpu.VMEM((members, cap), jnp.int32),
            pltpu.VMEM((members, cap), jnp.int32),
            pltpu.VMEM((members, cap), F32),
            pltpu.VMEM((1, members), jnp.int32),
            pltpu.VMEM((ITERS, members, cap), jnp.int32),
            pltpu.VMEM((1, slots), F32),
            pltpu.VMEM((1, slots), F32),
            pltpu.VMEM((ITERS, 4, slots), F32),
            pltpu.VMEM((ITERS, 4, slots), F32),
            pltpu.VMEM((ITERS, 2, slots), F32),
            pltpu.VMEM((ITERS, 2, slots), F32),
            pltpu.VMEM((ITERS, 2, ROWS, LANES), F32),
            pltpu.VMEM((ITERS + 1, 3, rows, cols), F32),
            pltpu.VMEM((rows, cols), F32),
            pltpu.VMEM((ITERS + 1, 2, seg_rows, LANES), F32),
            pltpu.VMEM((ITERS, 2, 3, ROWS, LANES), F32),
            pltpu.VMEM((ITERS, 2, 3, ROWS, cols), F32),
            pltpu.VMEM((ITERS, 6, 3, ROWS, LANES), F32),
            pltpu.VMEM((cols, slots), BF16),
            pltpu.VMEM((rows, slots), BF16),
            pltpu.VMEM((LANES, slots), BF16),
            pltpu.VMEM((seg_rows, slots), BF16),
            pltpu.VMEM((4 * rows, cols), F32),
            pltpu.VMEM((2 * rows, cols), F32),
            pltpu.VMEM((6 * seg_rows, LANES), F32),
            pltpu.VMEM((rows, cols), F32),
            pltpu.VMEM((rows + 2 * ROWS, cols + LANES), F32),
            pltpu.VMEM((rows + 2 * ROWS, cols + LANES), F32),
            pltpu.VMEM((rows + 2 * ROWS, cols + LANES), F32),
            dma(()),
            dma((lines,)),
            dma((ITERS,)),
            dma((ITERS,)),
            dma((ITERS,)),
            dma((ITERS, lines)),
            dma((ITERS,)),
            dma((ITERS,)),
            dma((ITERS, 2)),
            dma((ITERS, 2)),
            dma((10,)),
        ],
        compiler_params=pltpu.CompilerParams(
            collective_id=0, has_side_effects=True, vmem_limit_bytes=40 * 1024 * 1024
        ),
    )(
        *(
            pltpu.with_memory_space_constraint(x, pltpu.HBM)
            for x in (
                matrix_state,
                matrix_perm,
                frac_state.reshape(2, seg_rows, LANES),
                frac_aperture.reshape(seg_rows, LANES),
                link_cell[0, 0],
                link_seg[0, 0],
                link_trans[0, 0],
                link_count[0],
                link_upwind[:, 0, 0],
            )
        )
    )
    matrix_out, frac_out = pl.pallas_call(
        write_out,
        out_shape=(
            jax.ShapeDtypeStruct(matrix_state.shape, F32),
            jax.ShapeDtypeStruct((2, seg_rows, LANES), F32),
        ),
        in_specs=[vmem] * 2,
        out_specs=(hbm, hbm),
        scratch_shapes=[dma((2,))],
        compiler_params=pltpu.CompilerParams(vmem_limit_bytes=4 * 1024 * 1024),
    )(matrix_out, frac_out)
    return matrix_out, frac_out.reshape(2, 1, segs)


def solution(mesh):
    return jax.shard_map(
        on_device,
        mesh=mesh,
        in_specs=(
            P(None, "grp", "frac"),
            P("grp", "frac"),
            P(None, "grp", "frac"),
            P("grp", "frac"),
            P("grp", "frac", None, None),
            P("grp", "frac", None, None),
            P("grp", "frac", None, None),
            P("grp", "frac", None),
            P(None, "grp", "frac", None, None),
        ),
        out_specs=(P(None, "grp", "frac"), P(None, "grp", "frac")),
        check_vma=False,
    )
```
